256 devices in a mesh: dp: 4 (over y_lo, core), shard: 64 (over z, x, y_hi).
Axes of the slice: x: 4, y: 4 (y_hi: 2, y_lo: 2; y = y_hi * 2 + y_lo), z: 8, core: 2. Of those that a mesh axis runs over, the one named last changes fastest.
Arguments:
- grad_parts: bfloat16 [4, 14336, 2048], P('dp', 'shard'), may hold values from -6 to 6
- coarse_weight: float32 [14336, 2048], P('shard', 'dp'), may hold values from -6 to 6
- first_moment: float32 [14336, 2048], P('shard', 'dp'), may hold values from -6 to 6
- second_moment: float32 [14336, 2048], P('shard', 'dp'), may hold values from 0.05 to 4
- partner_device: int32 [28672, 1], P('shard'), may hold values from 0 to 63; in each aligned block of 448 rows (0 to 447, 448 to 895, ...) at most 14 rows name the same one
- partner_column: int32 [28672], P('shard'), may hold values from 0 to 223
Outputs:
- fine_weight: float32 [28672, 4096], P('shard', 'dp')
- fine_first: float32 [28672, 4096], P('shard', 'dp')
- fine_second: float32 [28672, 4096], P('shard', 'dp')
The draws below stay inside these ranges and needn't reach their ends.
Inputs may be any that keep to these rules, and one draw needn't show every extreme that they name: `partner_device`: within each aligned block of 28672 / 64 fine hidden units, no shard index is named more than 14 times, a bound that some block reaches.
All inputs are finite; a program needn't handle non-finite values.
Results may differ from the reference program's by a relative error of at most 0.0003.
Values sent between devices are 32-bit elements; how exact they have to be, the bound alone decides.
No kernel may reach another device: no remote copies, remote signals or barrier semaphores. Data moves between devices by JAX's collectives and lax.ppermute only.
A program may use at most 64 MiB of HBM per device.

```python
import math
import jax
import jax.numpy as jnp
import numpy as np
from jax import lax

DC = 2048
FC = 14336
STEP = 20
F = 28672
CAP = 14
N_DP = 4
N_SHARD = 64


def set_ends(array, key, low, top_value):
    shape = array.shape
    spot = [jax.random.randint(jax.random.fold_in(key, axis), (), 0, shape[axis]) for axis in range(len(shape))]
    array = array.at[tuple(spot)].set(low)
    longest = shape.index(max(shape))
    spot[longest] = (spot[longest] + 1) % shape[longest]
    return array.at[tuple(spot)].set(top_value)


def shard_levels(rng, dims, pieces, smallest, high):
    def one(axis_at, shards_of):
        steps = jax.random.uniform(jax.random.fold_in(jax.random.fold_in(rng, 6), axis_at), (shards_of,), jnp.float32, smallest / len(pieces), high / len(pieces))
        return jnp.repeat(jnp.exp(steps), dims[axis_at] // shards_of).reshape((-1,) + (1,) * (len(dims) - axis_at - 1))

    gain = one(*pieces[0])
    for cut in pieces[1:]:
        gain = gain * one(*cut)
    return gain


def deal_out(key, own, number, rows, amount, top, reach, slope):
    sequence = jax.random.permutation(key, amount)
    packed, common = shares(amount, rows * top, reach, slope, True), shares(amount, rows * top, reach, slope, False)
    places = jnp.arange(amount)

    def named(tallies, turn):
        used = int((tallies > 0).sum())
        fixed = max(1, used // 4)
        shifted = fixed + (places - fixed + turn * (used - fixed)) % max(1, amount - fixed)
        return jnp.zeros((amount,), jnp.int32).at[sequence[jnp.where(places < fixed, places, shifted)]].set(jnp.asarray(tallies, jnp.int32))

    tallies = jnp.where(number % 4 == 0, named(packed, number // 4), named(common, number - number // 4 - 1))
    mixed = jax.random.permutation(jax.random.fold_in(own, 3), amount)
    donor, receiver = mixed[0:amount // 2 * 2:2], mixed[1:amount // 2 * 2:2]
    margin = jnp.minimum(tallies[donor] - 1, reach - tallies[receiver]) // 2
    margin = jnp.where((donor == sequence[0]) | (receiver == sequence[0]) | (tallies[receiver] == 0), 0, jnp.maximum(margin, 0))
    shifted = jax.random.randint(jax.random.fold_in(own, 4), (amount // 2,), 0, 1 << 20) % (margin + 1)
    tallies = tallies.at[donor].add(-shifted).at[receiver].add(shifted)
    items = jnp.searchsorted(jnp.cumsum(tallies), jnp.arange(rows * top), side="right").astype(jnp.int32)
    table = items.reshape(top, rows).T
    table = table[jax.random.permutation(jax.random.fold_in(own, 1), rows)]
    turn = jax.random.randint(jax.random.fold_in(own, 2), (rows, 1), 0, top)
    return jnp.take_along_axis(table, (jnp.arange(top)[None, :] + turn) % top, axis=1)


def shares(count, total, limit, skew, full):
    weights = [(1 << 20) // math.isqrt(rank ** skew) + 1 for rank in range(1, count + 1)]
    largest = limit if full else min(limit, max(-(-total // count), total * weights[0] // sum(weights)))
    least = 1 if total - largest >= count - 1 else 0
    counts, spare = [largest] + [least] * (count - 1), total - largest - least * (count - 1)
    while spare > 0:
        candidates = [i for i in range(1, count) if counts[i] < largest] or [i for i in range(1, count) if counts[i] < limit]
        mass, remaining = sum([weights[i] for i in candidates]), spare
        for i in candidates:
            addition = min(limit - counts[i], max(1, remaining * weights[i] // mass), spare)
            counts[i] = counts[i] + addition
            spare = spare - addition
    return np.array(counts)


def noise(rng, shape, scale, reach, split=(), kind=jnp.bfloat16):
    values = scale * jax.random.normal(rng, shape, jnp.float32)
    if split:
        values = values * shard_levels(rng, shape, split, -0.22, 0.18)
    return jnp.clip(values, -reach, reach).astype(kind)


def setup_inputs(seed: int = 0) -> dict:
    streams_of = jax.random.split(jax.random.key(seed), 7)
    grad_parts = noise(streams_of[0], (N_DP, FC, DC), 1.0, 6.0, ((0, 4), (1, 64)))
    coarse_weight = noise(streams_of[1], (FC, DC), 1.0, 6.0, ((0, 64), (1, 4)), jnp.float32)
    first_moment = noise(streams_of[2], (FC, DC), 1.0, 6.0, ((0, 64), (1, 4)), jnp.float32)
    second_moment = jnp.clip(jnp.exp(math.log(4.0) - 4.3820266 * jax.random.uniform(streams_of[3], (FC, DC), jnp.float32) ** shard_levels(streams_of[3], (FC, DC), ((0, 64), (1, 4)), -0.2, 0.2)), 0.05, 4.0)
    partner_device_keys = jax.random.split(jax.random.fold_in(streams_of[4], 1), F // (F // N_SHARD))
    partner_device_turns = jax.random.permutation(jax.random.fold_in(streams_of[4], 3), F // (F // N_SHARD))
    partner_device = jax.vmap(lambda own, number: deal_out(jax.random.fold_in(streams_of[4], 2), own, number, F // N_SHARD, N_SHARD, 1, CAP, 1))(partner_device_keys, partner_device_turns).reshape((F, 1))
    partner_column = set_ends(jax.random.randint(streams_of[5], (F,), 0, FC // N_SHARD), jax.random.fold_in(streams_of[5], 1), 0, (FC // N_SHARD) - 1).astype(jnp.int32)
    return dict(grad_parts=grad_parts, coarse_weight=coarse_weight, first_moment=first_moment, second_moment=second_moment, partner_device=partner_device, partner_column=partner_column)


first_decay = 0.9
second_decay = 0.95
learning_rate = 0.02
weight_decay = 0.1
epsilon = 1e-08
own_share = 0.75

def adamw_update(weight, first, second, grad):
    new_first = first_decay * first + (1.0 - first_decay) * grad
    new_second = second_decay * second + (1.0 - second_decay) * grad * grad
    first_hat = new_first / (1.0 - first_decay ** STEP)
    second_hat = new_second / (1.0 - second_decay ** STEP)
    new_weight = weight - learning_rate * (first_hat / (jnp.sqrt(second_hat) + epsilon) + weight_decay * weight)
    return (new_weight, new_first, new_second)

def reference(grad_parts, coarse_weight, first_moment, second_moment, partner_device, partner_column):
    grad = lax.optimization_barrier(jnp.sum(grad_parts.astype(jnp.float32), axis=0))
    new_weight, new_first, new_second = adamw_update(coarse_weight, first_moment, second_moment, grad)
    partner = (partner_device[:, 0] * (FC // N_SHARD) + partner_column).astype(jnp.int32)
    source = (jnp.arange(F) // 2).astype(jnp.int32)

    def expand(state):
        mixed = own_share * state[source] + (1.0 - own_share) * state[partner]
        return jnp.repeat(mixed, 2, axis=1)
    return (expand(new_weight), expand(new_first), expand(new_second))
```

```python
import jax
import jax.numpy as jnp
from jax import lax
from jax.experimental import pallas as pl
from jax.experimental.pallas import tpu as pltpu
from jax.sharding import PartitionSpec as P

STEP = 20

first_decay = 0.9
second_decay = 0.95
learning_rate = 0.02
weight_decay = 0.1
epsilon = 1e-08
own_share = 0.75

F32 = jnp.float32
BF16 = jnp.bfloat16
I32 = jnp.int32

ROWS = 224
FINE = 448
FEATS = 512
HALF = 256
WIDE = 3 * HALF
SLOTS = 16
PLANE = 8
RING = 8

VMEM = pltpu.CompilerParams(vmem_limit_bytes=48 * 1024 * 1024)


def call(kernel, out, *, grid=None, in_specs=None, out_specs=None, flops=0, moved=0):
    extra = {}
    if grid is not None:
        extra = dict(grid=grid, in_specs=in_specs, out_specs=out_specs)
    elif in_specs is not None:
        extra = dict(in_specs=in_specs)
    return pl.pallas_call(
        kernel,
        out_shape=out,
        compiler_params=VMEM,
        cost_estimate=pl.CostEstimate(flops=flops, bytes_accessed=moved, transcendentals=0),
        **extra,
    )


def whole():
    return pl.BlockSpec(memory_space=pltpu.VMEM)


def scalar():
    return pl.BlockSpec(memory_space=pltpu.SMEM)


def split_dot(chosen, values, contract=((1,), (0,))):
    high = values.astype(BF16)
    low = (values - high.astype(F32)).astype(BF16)
    dims = (contract, ((), ()))
    return lax.dot_general(chosen, high, dims, preferred_element_type=F32) + lax.dot_general(
        chosen, low, dims, preferred_element_type=F32
    )


def send_core_kernel(place, grad, out0, out1):
    dp = place[1]
    core, y = lax.rem(dp, 2), lax.div(dp, 2)
    for half, out in enumerate((out0, out1)):
        for part, row in enumerate((1 - y, y)):
            at = pl.multiple_of((row * 2 + 1 - core) * FEATS + half * HALF, HALF)
            out[:, part * HALF : (part + 1) * HALF] = grad[:, pl.ds(at, HALF)].astype(F32)


def send_y_kernel(half, place, grad, got, out):
    dp = place[1]
    core, y = lax.rem(dp, 2), lax.div(dp, 2)
    at = pl.multiple_of(((1 - y) * 2 + core) * FEATS + half * HALF, HALF)
    out[...] = grad[:, pl.ds(at, HALF)].astype(F32) + got[...]


def update_kernel(half, place, grad, got, got_y, weight, first, second, out):
    dp = place[1]
    at = pl.multiple_of(dp * FEATS + half * HALF, HALF)
    total = grad[:, pl.ds(at, HALF)].astype(F32) + got[...] + got_y[...]
    new_first = first_decay * first[...] + (1.0 - first_decay) * total
    new_second = second_decay * second[...] + (1.0 - second_decay) * total * total
    first_hat = new_first / (1.0 - first_decay**STEP)
    second_hat = new_second / (1.0 - second_decay**STEP)
    old = weight[...]
    new_weight = old - learning_rate * (
        first_hat / (jnp.sqrt(second_hat) + epsilon) + weight_decay * old
    )
    out[:, 0:HALF] = new_weight
    out[:, HALF : 2 * HALF] = new_first
    out[:, 2 * HALF : 3 * HALF] = new_second


def index_kernel(place, dev, dev_row, col, wanted, codes):
    shard = place[0]
    plane, me = lax.div(shard, PLANE), lax.rem(shard, PLANE)
    d = dev[...]
    r = dev_row[...]
    earlier = lax.broadcasted_iota(I32, (FINE, FINE), 1) < lax.broadcasted_iota(
        I32, (FINE, FINE), 0
    )
    slot = jnp.sum(jnp.where(earlier & (d == r), 1, 0), axis=1, keepdims=True)
    source_xy, source_z = d & (PLANE - 1), d >> 3
    row_of = ((r & (PLANE - 1)) << 3) + (r >> 3)
    left = jnp.where(lax.broadcasted_iota(I32, (64, FINE), 0) == row_of, 1.0, 0.0).astype(BF16)
    right = jnp.where(
        lax.broadcasted_iota(I32, (FINE, 128), 1) == me * SLOTS + slot, col[...].astype(F32), 0.0
    ).astype(BF16)
    table = jnp.dot(left, right, preferred_element_type=F32)
    wanted[...] = table.astype(I32).reshape(PLANE, RING, 128)
    away = (source_z - plane + RING) & (RING - 1)
    none = -1

    def place_in(rows, offsets):
        at = jnp.full((FINE, 1), none, I32)
        for k, offset in offsets:
            at = jnp.where(away == k, source_xy * rows + offset + slot, at)
        return at

    groups = (
        place_in(48, ((0, 0), (7, 16), (1, 32))),
        place_in(32, ((6, 0), (2, 16))),
        place_in(32, ((5, 0), (3, 16))),
        place_in(16, ((4, 0),)),
    )
    lane = lax.broadcasted_iota(I32, (FINE, 128), 1)
    out = jnp.full((FINE, 128), none, I32)
    for g, at in enumerate(groups):
        out = jnp.where(lane == g, at, out)
    codes[...] = out


def asked_rows(asked, plane):
    table = jnp.sum(asked[...], axis=0)
    here = lax.broadcasted_iota(I32, (RING, 128), 0) == plane
    return jnp.sum(jnp.where(here, table, 0), axis=0, keepdims=True)


def pick_from(asked, plane, values):
    rows = values.shape[0]
    chosen = jnp.where(
        lax.broadcasted_iota(I32, (rows, 128), 0) == asked_rows(asked, plane), 1.0, 0.0
    ).astype(BF16)
    return split_dot(chosen, values, ((0,), (0,)))


def pick_kernel(offsets, place, asked, *refs):
    out = refs[-1]
    plane = lax.div(place[0], PLANE)
    for n, offset in enumerate(offsets):
        from_plane = (plane + offset + RING) & (RING - 1)
        for half in range(2):
            got = pick_from(asked, from_plane, refs[2 * n + half][...])
            for d in range(PLANE):
                out[d, n * SLOTS : (n + 1) * SLOTS, half * WIDE : (half + 1) * WIDE] = got[
                    d * SLOTS : (d + 1) * SLOTS
                ]


def pick_last_kernel(place, asked, low0, low1, high0, high1, out):
    plane = lax.div(place[0], PLANE)
    from_plane = (plane + 4) & (RING - 1)
    for half, (low, high) in enumerate(((low0, high0), (low1, high1))):
        got = pick_from(asked, from_plane, jnp.concatenate([low[...], high[...]], axis=0))
        for d in range(PLANE):
            out[d, :, half * WIDE : (half + 1) * WIDE] = got[d * SLOTS : (d + 1) * SLOTS]


def far_dot(codes, group, far):
    rows = far.shape[0] * far.shape[1]
    at = codes[:, group : group + 1]
    chosen = jnp.where(
        lax.broadcasted_iota(I32, (FINE, rows), 1) == at, 1.0 - own_share, 0.0
    ).astype(BF16)
    return split_dot(chosen, far[...].reshape(rows, far.shape[2]))


def gather_kernel(codes, near0, near1, far1, far2, out):
    i = pl.program_id(0)
    near = jnp.where(i < 3, near0[...], near1[...])
    own = lax.broadcasted_iota(I32, (FINE, ROWS), 0) >> 1
    chosen = jnp.where(
        lax.broadcasted_iota(I32, (FINE, ROWS), 1) == own, own_share, 0.0
    ).astype(BF16)
    out[...] = split_dot(chosen, near) + far_dot(codes, 0, far1) + far_dot(codes, 1, far2)


def final_kernel(codes, *refs):
    lane = lax.broadcasted_iota(I32, (FINE, 128), 1) >> 1
    for state in range(3):
        acc, far3, far4 = refs[state], refs[3 + state], refs[6 + state]
        out = refs[9 + state]
        mixed = acc[...] + far_dot(codes, 2, far3) + far_dot(codes, 3, far4)
        out[:, 0:128] = jnp.take_along_axis(mixed, lane, axis=1)
        out[:, 128:256] = jnp.take_along_axis(mixed, lane + 64, axis=1)


PLANES = [[z * PLANE + p for p in range(PLANE)] for z in range(RING)]
UP = [(z * PLANE + p, ((z + 1) % RING) * PLANE + p) for z in range(RING) for p in range(PLANE)]
DOWN = [(b, a) for a, b in UP]
CORE = [(0, 1), (1, 0), (2, 3), (3, 2)]
NEXT_Y = [(0, 2), (2, 0), (1, 3), (3, 1)]


def shape(*dims, dtype=F32):
    return jax.ShapeDtypeStruct(dims, dtype)


def on_device(grad_parts, weight, first, second, partner_device, partner_column):
    place = jnp.stack([lax.axis_index("shard"), lax.axis_index("dp")]).astype(I32)
    grad = grad_parts[0]

    sends = call(
        send_core_kernel,
        (shape(ROWS, 2 * HALF),) * 2,
        in_specs=[scalar(), whole()],
        moved=3 << 20,
    )(place, grad)
    got_core = [lax.ppermute(s, "dp", CORE) for s in sends]
    state = []
    for half in range(2):
        got = got_core[half]
        passed = call(
            lambda *refs, half=half: send_y_kernel(half, *refs),
            shape(ROWS, HALF),
            grid=(1,),
            in_specs=[
                scalar(),
                pl.BlockSpec((ROWS, 4 * FEATS), lambda i: (0, 0)),
                pl.BlockSpec((ROWS, HALF), lambda i: (0, 0)),
            ],
            out_specs=pl.BlockSpec((ROWS, HALF), lambda i: (0, 0)),
            moved=1 << 20,
        )(place, grad, got)
        got_y = lax.ppermute(passed, "dp", NEXT_Y)
        block = pl.BlockSpec((ROWS, HALF), lambda i, half=half: (0, half))
        state.append(
            call(
                lambda *refs, half=half: update_kernel(half, *refs),
                shape(ROWS, WIDE),
                grid=(1,),
                in_specs=[
                    scalar(),
                    pl.BlockSpec((ROWS, 4 * FEATS), lambda i: (0, 0)),
                    pl.BlockSpec((ROWS, HALF), lambda i: (0, 1)),
                    pl.BlockSpec((ROWS, HALF), lambda i: (0, 0)),
                    block,
                    block,
                    block,
                ],
                out_specs=pl.BlockSpec((ROWS, WIDE), lambda i: (0, 0)),
                moved=2 << 20,
            )(place, grad, got, got_y, weight, first, second)
        )

    wanted, codes = call(
        index_kernel,
        (shape(PLANE, RING, 128, dtype=I32), shape(FINE, 128, dtype=I32)),
        in_specs=[scalar(), whole(), whole(), whole()],
        moved=1 << 20,
    )(
        place,
        partner_device,
        partner_device.reshape(1, FINE),
        partner_column.reshape(FINE, 1),
    )
    asked = lax.all_to_all(
        wanted, "shard", split_axis=0, concat_axis=0, axis_index_groups=PLANES, tiled=True
    )

    up, down = [state], [state]
    for step in range(3):
        nu, nd = [], []
        for half in range(2):
            nu.append(lax.ppermute(up[-1][half], "shard", UP))
            nd.append(lax.ppermute(down[-1][half], "shard", DOWN))
        up.append(nu)
        down.append(nd)
    middle = ROWS // 2
    low = [lax.ppermute(up[3][half][:middle], "shard", UP) for half in range(2)]
    high = [lax.ppermute(down[3][half][middle:], "shard", DOWN) for half in range(2)]

    def pick(offsets, sources):
        rows = SLOTS * len(offsets)
        return call(
            lambda *refs: pick_kernel(offsets, *refs),
            shape(PLANE, rows, 2 * WIDE),
            in_specs=[scalar()] + [whole()] * (1 + len(sources)),
            flops=rows * PLANE * ROWS * WIDE * 8,
            moved=(len(sources) + 2) << 20,
        )(place, asked, *sources)

    def to_plane(rows):
        return lax.all_to_all(
            rows, "shard", split_axis=0, concat_axis=0, axis_index_groups=PLANES, tiled=True
        )

    far1 = to_plane(pick((0, -1, 1), (*state, *up[1], *down[1])))
    far2 = to_plane(pick((-2, 2), (*up[2], *down[2])))
    far3 = to_plane(pick((-3, 3), (*up[3], *down[3])))
    last = call(
        pick_last_kernel,
        shape(PLANE, SLOTS, 2 * WIDE),
        in_specs=[scalar()] + [whole()] * 5,
        flops=SLOTS * PLANE * ROWS * WIDE * 8,
        moved=3 << 20,
    )(place, asked, *low, *high)
    far4 = to_plane(last)

    acc = call(
        gather_kernel,
        shape(FINE, 2 * WIDE),
        grid=(6,),
        in_specs=[
            pl.BlockSpec((FINE, 128), lambda i: (0, 0)),
            pl.BlockSpec((ROWS, HALF), lambda i: (0, jnp.minimum(i, 2))),
            pl.BlockSpec((ROWS, HALF), lambda i: (0, jnp.maximum(i - 3, 0))),
            pl.BlockSpec((PLANE, 48, HALF), lambda i: (0, 0, i)),
            pl.BlockSpec((PLANE, 32, HALF), lambda i: (0, 0, i)),
        ],
        out_specs=pl.BlockSpec((FINE, HALF), lambda i: (0, i)),
        flops=FINE * 864 * 1536 * 4,
        moved=8 << 20,
    )(codes, *state, far1, far2)

    def lanes(block, state):
        n = len(block) - 1
        return pl.BlockSpec(
            block, lambda j: (0,) * n + (lax.div(j, 2) * 6 + state * 2 + lax.rem(j, 2),)
        )

    return call(
        final_kernel,
        (shape(FINE, 2 * FEATS),) * 3,
        grid=(4,),
        in_specs=[pl.BlockSpec((FINE, 128), lambda j: (0, 0))]
        + [lanes((FINE, 128), s) for s in range(3)]
        + [lanes((PLANE, 32, 128), s) for s in range(3)]
        + [lanes((PLANE, 16, 128), s) for s in range(3)],
        out_specs=(pl.BlockSpec((FINE, 256), lambda j: (0, j)),) * 3,
        flops=FINE * 384 * 1536 * 4,
        moved=12 << 20,
    )(codes, acc, acc, acc, far3, far3, far3, far4, far4, far4)


def solution(mesh):
    placed = (
        P("dp", "shard", None),
        P("shard", "dp"),
        P("shard", "dp"),
        P("shard", "dp"),
        P("shard", None),
        P("shard"),
    )
    return jax.shard_map(
        on_device,
        mesh=mesh,
        in_specs=placed,
        out_specs=(P("shard", "dp"), P("shard", "dp"), P("shard", "dp")),
        check_vma=False,
    )
```

```python
import jax
import jax.numpy as jnp
from jax import lax
from jax.experimental import pallas as pl
from jax.experimental.pallas import tpu as pltpu
from jax.sharding import PartitionSpec as P

STEP = 20

first_decay = 0.9
second_decay = 0.95
learning_rate = 0.02
weight_decay = 0.1
epsilon = 1e-08
own_share = 0.75

F32 = jnp.float32
BF16 = jnp.bfloat16
I32 = jnp.int32

ROWS = 224
FINE = 448
FEATS = 512
HALF = 256
WIDE = 3 * HALF
SLOTS = 16
PLANE = 8
RING = 8

VMEM = pltpu.CompilerParams(vmem_limit_bytes=48 * 1024 * 1024)


def call(kernel, out, *, grid=None, in_specs=None, out_specs=None, flops=0, moved=0):
    extra = {}
    if grid is not None:
        extra = dict(grid=grid, in_specs=in_specs, out_specs=out_specs)
    elif in_specs is not None:
        extra = dict(in_specs=in_specs)
    return pl.pallas_call(
        kernel,
        out_shape=out,
        compiler_params=VMEM,
        cost_estimate=pl.CostEstimate(flops=flops, bytes_accessed=moved, transcendentals=0),
        **extra,
    )


def shape(*dims, dtype=F32):
    return jax.ShapeDtypeStruct(dims, dtype)


def whole():
    return pl.BlockSpec(memory_space=pltpu.VMEM)


def scalar():
    return pl.BlockSpec(memory_space=pltpu.SMEM)


def split_dot(chosen, values, contract=((1,), (0,))):
    high = values.astype(BF16)
    low = (values - high.astype(F32)).astype(BF16)
    dims = (contract, ((), ()))
    return lax.dot_general(chosen, high, dims, preferred_element_type=F32) + lax.dot_general(
        chosen, low, dims, preferred_element_type=F32
    )


def send_core_kernel(place, grad, out0, out1):
    dp = place[1]
    core, y = lax.rem(dp, 2), lax.div(dp, 2)
    for half, out in enumerate((out0, out1)):
        for part, row in enumerate((1 - y, y)):
            at = pl.multiple_of((row * 2 + 1 - core) * FEATS + half * HALF, HALF)
            out[:, part * HALF : (part + 1) * HALF] = grad[:, pl.ds(at, HALF)].astype(F32)


def send_y_kernel(half, place, grad, got, out):
    dp = place[1]
    core, y = lax.rem(dp, 2), lax.div(dp, 2)
    at = pl.multiple_of(((1 - y) * 2 + core) * FEATS + half * HALF, HALF)
    out[...] = grad[:, pl.ds(at, HALF)].astype(F32) + got[...]


def update_kernel(half, place, grad, got, got_y, weight, first, second, out):
    dp = place[1]
    at = pl.multiple_of(dp * FEATS + half * HALF, HALF)
    total = grad[:, pl.ds(at, HALF)].astype(F32) + got[...] + got_y[...]
    new_first = first_decay * first[...] + (1.0 - first_decay) * total
    new_second = second_decay * second[...] + (1.0 - second_decay) * total * total
    first_hat = new_first / (1.0 - first_decay**STEP)
    second_hat = new_second / (1.0 - second_decay**STEP)
    old = weight[...]
    new_weight = old - learning_rate * (
        first_hat / (jnp.sqrt(second_hat) + epsilon) + weight_decay * old
    )
    out[:, 0:HALF] = new_weight
    out[:, HALF : 2 * HALF] = new_first
    out[:, 2 * HALF : 3 * HALF] = new_second


def index_kernel(place, dev, dev_row, col, wanted, codes):
    shard = place[0]
    plane, me = lax.div(shard, PLANE), lax.rem(shard, PLANE)
    d = dev[...]
    r = dev_row[...]
    earlier = lax.broadcasted_iota(I32, (FINE, FINE), 1) < lax.broadcasted_iota(
        I32, (FINE, FINE), 0
    )
    slot = jnp.sum(jnp.where(earlier & (d == r), 1, 0), axis=1, keepdims=True)
    source_xy, source_z = d & (PLANE - 1), d >> 3
    row_of = ((r & (PLANE - 1)) << 3) + (r >> 3)
    left = jnp.where(lax.broadcasted_iota(I32, (64, FINE), 0) == row_of, 1.0, 0.0).astype(BF16)
    right = jnp.where(
        lax.broadcasted_iota(I32, (FINE, 128), 1) == me * SLOTS + slot, col[...].astype(F32), 0.0
    ).astype(BF16)
    table = jnp.dot(left, right, preferred_element_type=F32)
    wanted[...] = table.astype(I32).reshape(PLANE, RING, 128)
    away = (source_z - plane + RING) & (RING - 1)
    none = -1

    def place_in(offsets):
        at = jnp.full((FINE, 1), none, I32)
        for k, offset in offsets:
            at = jnp.where(away == k, source_xy * 64 + offset + slot, at)
        return at

    groups = (
        place_in(((0, 0), (7, 32), (1, 48))),
        place_in(((6, 32), (2, 48))),
        place_in(((5, 32), (3, 48))),
        place_in(((4, 32),)),
        place_in(((0, 16),)),
        place_in(((7, 0), (1, 16))),
        place_in(((6, 0), (2, 16))),
        place_in(((5, 0), (3, 16), (4, 48))),
    )
    lane = lax.broadcasted_iota(I32, (FINE, 128), 1)
    out = jnp.full((FINE, 128), none, I32)
    for g, at in enumerate(groups):
        out = jnp.where(lane == g, at, out)
    codes[...] = out


def asked_rows(asked, plane):
    table = jnp.sum(asked[...], axis=0)
    here = lax.broadcasted_iota(I32, (RING, 128), 0) == plane
    return jnp.sum(jnp.where(here, table, 0), axis=0, keepdims=True)


def pick_from(asked, plane, values):
    rows = values.shape[0]
    chosen = jnp.where(
        lax.broadcasted_iota(I32, (rows, 128), 0) == asked_rows(asked, plane), 1.0, 0.0
    ).astype(BF16)
    return split_dot(chosen, values, ((0,), (0,)))


def pick_kernel(parts, place, asked, *refs):
    out = refs[-1]
    plane = lax.div(place[0], PLANE)
    n = 0
    for away, row, pieces in parts:
        values = refs[n][...]
        if pieces == 2:
            values = jnp.concatenate([values, refs[n + 1][...]], axis=0)
        n += pieces
        got = pick_from(asked, (plane + away + RING) & (RING - 1), values)
        for d in range(PLANE):
            out[d, row : row + SLOTS, :] = got[d * SLOTS : (d + 1) * SLOTS]


def held_kernel(*refs):
    pass


def hold(arrays, *until):
    n = len(arrays)
    return pl.pallas_call(
        held_kernel,
        out_shape=tuple(shape(*a.shape) for a in arrays),
        in_specs=[pl.BlockSpec(memory_space=pl.ANY)] * (n + len(until)),
        out_specs=(pl.BlockSpec(memory_space=pl.ANY),) * n,
        input_output_aliases={i: i for i in range(n)},
        cost_estimate=pl.CostEstimate(flops=0, bytes_accessed=1 << 20, transcendentals=0),
    )(*arrays, *until)


def token_kernel(*refs):
    refs[-1][...] = jnp.zeros((8, 128), F32)


def token(arrays):
    return call(
        token_kernel,
        shape(8, 128),
        in_specs=[pl.BlockSpec(memory_space=pl.ANY)] * len(arrays),
        flops=10**10,
    )(*arrays)


def far_dot(at, far):
    rows = far.shape[0] * far.shape[1]
    chosen = jnp.where(
        lax.broadcasted_iota(I32, (FINE, rows), 1) == at, 1.0 - own_share, 0.0
    ).astype(BF16)
    return split_dot(chosen, far.reshape(rows, far.shape[2]))


def far_part(codes, lane, far, low, high):
    at = codes[:, lane : lane + 1]
    xy, row = at >> 6, at & 63
    here = (at >= 0) & (row >= low) & (row < high)
    at = jnp.where(here, xy * (high - low) + row - low, -1)
    return far_dot(at, far[:, low:high, :])


def gather_kernel(parts, codes, near, far1, far2, far3, out):
    own = lax.broadcasted_iota(I32, (FINE, ROWS), 0) >> 1
    chosen = jnp.where(
        lax.broadcasted_iota(I32, (FINE, ROWS), 1) == own, own_share, 0.0
    ).astype(BF16)
    total = split_dot(chosen, near[...])
    far = (far1, far2, far3)
    for lane, exchange, low, high in parts:
        total = total + far_part(codes, lane, far[exchange], low, high)
    out[...] = total


def final_kernel(codes, *refs):
    lane = lax.broadcasted_iota(I32, (FINE, 128), 1) >> 1
    first_half = pl.program_id(0) < 2
    at = jnp.where(first_half, codes[:, 3:4], codes[:, 7:8])
    for state in range(3):
        acc0, acc1, far, out = (refs[3 * k + state] for k in range(4))
        acc = jnp.where(first_half, acc0[...], acc1[...])
        mixed = acc + far_dot(at, far[...])
        out[:, 0:128] = jnp.take_along_axis(mixed, lane, axis=1)
        out[:, 128:256] = jnp.take_along_axis(mixed, lane + 64, axis=1)


PLANES = [[z * PLANE + p for p in range(PLANE)] for z in range(RING)]
UP = [(z * PLANE + p, ((z + 1) % RING) * PLANE + p) for z in range(RING) for p in range(PLANE)]
DOWN = [(b, a) for a, b in UP]
CORE = [(0, 1), (1, 0), (2, 3), (3, 2)]
NEXT_Y = [(0, 2), (2, 0), (1, 3), (3, 1)]


def on_device(grad_parts, weight, first, second, partner_device, partner_column):
    place = jnp.stack([lax.axis_index("shard"), lax.axis_index("dp")]).astype(I32)
    grad = grad_parts[0]

    sends = call(
        send_core_kernel,
        (shape(ROWS, 2 * HALF),) * 2,
        in_specs=[scalar(), whole()],
        moved=3 << 20,
    )(place, grad)
    got_core = [lax.ppermute(s, "dp", CORE) for s in sends]
    state = []
    for half in range(2):
        got = got_core[half]
        passed = call(
            lambda *refs, half=half: send_y_kernel(half, *refs),
            shape(ROWS, HALF),
            grid=(1,),
            in_specs=[
                scalar(),
                pl.BlockSpec((ROWS, 4 * FEATS), lambda i: (0, 0)),
                pl.BlockSpec((ROWS, HALF), lambda i: (0, 0)),
            ],
            out_specs=pl.BlockSpec((ROWS, HALF), lambda i: (0, 0)),
            moved=1 << 20,
        )(place, grad, got)
        got_y = lax.ppermute(passed, "dp", NEXT_Y)
        block = pl.BlockSpec((ROWS, HALF), lambda i, half=half: (0, half))
        state.append(
            call(
                lambda *refs, half=half: update_kernel(half, *refs),
                shape(ROWS, WIDE),
                grid=(1,),
                in_specs=[
                    scalar(),
                    pl.BlockSpec((ROWS, 4 * FEATS), lambda i: (0, 0)),
                    pl.BlockSpec((ROWS, HALF), lambda i: (0, 1)),
                    pl.BlockSpec((ROWS, HALF), lambda i: (0, 0)),
                    block,
                    block,
                    block,
                ],
                out_specs=pl.BlockSpec((ROWS, WIDE), lambda i: (0, 0)),
                moved=2 << 20,
            )(place, grad, got, got_y, weight, first, second)
        )

    wanted, codes = call(
        index_kernel,
        (shape(PLANE, RING, 128, dtype=I32), shape(FINE, 128, dtype=I32)),
        in_specs=[scalar(), whole(), whole(), whole()],
        moved=1 << 20,
    )(
        place,
        partner_device,
        partner_device.reshape(1, FINE),
        partner_column.reshape(FINE, 1),
    )
    asked = lax.all_to_all(
        wanted, "shard", split_axis=0, concat_axis=0, axis_index_groups=PLANES, tiled=True
    )

    def pick(parts, sources, after=()):
        return call(
            lambda *refs: pick_kernel(parts, *refs),
            shape(PLANE, SLOTS * len(parts), WIDE),
            in_specs=[scalar()]
            + [whole()] * (1 + len(sources))
            + [pl.BlockSpec(memory_space=pl.ANY)] * len(after),
            flops=len(parts) * SLOTS * PLANE * ROWS * WIDE * 4,
            moved=(len(sources) + 2) << 20,
        )(place, asked, *sources, *after)

    def to_plane(rows):
        return lax.all_to_all(
            rows, "shard", split_axis=0, concat_axis=0, axis_index_groups=PLANES, tiled=True
        )

    def around(pair):
        return lax.ppermute(pair[0], "shard", UP), lax.ppermute(pair[1], "shard", DOWN)

    one = [around((x, x)) for x in state]
    one[0] = hold(one[0], asked)
    two = [around(pair) for pair in one]
    three = [around(pair) for pair in two]
    far1 = to_plane(pick(((0, 0, 1), (0, 16, 1), (-1, 32, 1), (1, 48, 1)), (*state, *one[0])))
    far2 = to_plane(
        pick(((-1, 0, 1), (1, 16, 1), (-2, 32, 1), (2, 48, 1)), (*one[1], *two[0]), (far1, token(two[0])))
    )
    far3 = to_plane(
        pick(((-2, 0, 1), (2, 16, 1), (-3, 32, 1), (3, 48, 1)), (*two[1], *three[0]), (far2, token(three[0])))
    )
    middle = ROWS // 2
    four = [around((pair[0][:middle], pair[1][middle:])) for pair in three]
    rows = pick(
        ((-3, 0, 1), (3, 16, 1), (4, 32, 2), (4, 48, 2)), (*three[1], *four[0], *four[1]), (far3, token(four[1]))
    )
    far4 = to_plane(rows)

    acc = []
    for half, parts in enumerate(
        (
            ((0, 0, 0, 16), (0, 0, 32, 64), (1, 1, 32, 64), (2, 2, 32, 64)),
            ((4, 0, 16, 32), (5, 1, 0, 32), (6, 2, 0, 32)),
        )
    ):
        acc.append(
            call(
                lambda *refs, parts=parts: gather_kernel(parts, *refs),
                shape(FINE, WIDE),
                grid=(3,),
                in_specs=[
                    pl.BlockSpec((FINE, 128), lambda i: (0, 0)),
                    pl.BlockSpec((ROWS, HALF), lambda i: (0, i)),
                ]
                + [pl.BlockSpec((PLANE, 64, HALF), lambda i: (0, 0, i))] * 3,
                out_specs=pl.BlockSpec((FINE, HALF), lambda i: (0, i)),
                flops=FINE * 1120 * WIDE * 4,
                moved=8 << 20,
            )(codes, state[half], far1, far2, far3)
        )

    def acc_block(half, state):
        def index(j):
            k = jnp.minimum(j, 1) if half == 0 else jnp.maximum(j - 2, 0)
            return 0, state * 2 + k

        return pl.BlockSpec((FINE, 128), index)

    def far_block(state):
        return pl.BlockSpec((PLANE, 64, 128), lambda j: (0, 0, state * 2 + lax.rem(j, 2)))

    return call(
        final_kernel,
        (shape(FINE, 2 * FEATS),) * 3,
        grid=(4,),
        in_specs=[pl.BlockSpec((FINE, 128), lambda j: (0, 0))]
        + [acc_block(half, s) for half in range(2) for s in range(3)]
        + [far_block(s) for s in range(3)],
        out_specs=(pl.BlockSpec((FINE, 256), lambda j: (0, j)),) * 3,
        flops=FINE * 512 * 1536 * 4,
        moved=12 << 20,
    )(codes, acc[0], acc[0], acc[0], acc[1], acc[1], acc[1], far4, far4, far4)


def solution(mesh):
    placed = (
        P("dp", "shard", None),
        P("shard", "dp"),
        P("shard", "dp"),
        P("shard", "dp"),
        P("shard", None),
        P("shard"),
    )
    return jax.shard_map(
        on_device,
        mesh=mesh,
        in_specs=placed,
        out_specs=(P("shard", "dp"), P("shard", "dp"), P("shard", "dp")),
        check_vma=False,
    )
```

```python
import jax
import jax.numpy as jnp
from jax import lax
from jax.experimental import pallas as pl
from jax.experimental.pallas import tpu as pltpu
from jax.sharding import PartitionSpec as P

STEP = 20

first_decay = 0.9
second_decay = 0.95
learning_rate = 0.02
weight_decay = 0.1
epsilon = 1e-08
own_share = 0.75

F32 = jnp.float32
BF16 = jnp.bfloat16
I32 = jnp.int32

ROWS = 224
FINE = 448
FEATS = 512
HALF = 256
WIDE = 3 * HALF
SLOTS = 16
PLANE = 8
RING = 8

VMEM = pltpu.CompilerParams(vmem_limit_bytes=12 * 1024 * 1024)


def call(kernel, out, *, grid=None, in_specs=None, out_specs=None, flops=0, moved=0):
    extra = {}
    if grid is not None:
        extra = dict(grid=grid, in_specs=in_specs, out_specs=out_specs)
    elif in_specs is not None:
        extra = dict(in_specs=in_specs)
    return pl.pallas_call(
        kernel,
        out_shape=out,
        compiler_params=VMEM,
        cost_estimate=pl.CostEstimate(flops=flops, bytes_accessed=moved, transcendentals=0),
        **extra,
    )


def shape(*dims, dtype=F32):
    return jax.ShapeDtypeStruct(dims, dtype)


def whole():
    return pl.BlockSpec(memory_space=pltpu.VMEM)


def scalar():
    return pl.BlockSpec(memory_space=pltpu.SMEM)


def split_dot(chosen, values, contract=((1,), (0,))):
    high = values.astype(BF16)
    low = (values - high.astype(F32)).astype(BF16)
    dims = (contract, ((), ()))
    return lax.dot_general(chosen, high, dims, preferred_element_type=F32) + lax.dot_general(
        chosen, low, dims, preferred_element_type=F32
    )


def send_core_kernel(place, grad, out0, out1):
    dp = place[1]
    core, y = lax.rem(dp, 2), lax.div(dp, 2)
    for half, out in enumerate((out0, out1)):
        for part, row in enumerate((1 - y, y)):
            at = pl.multiple_of((row * 2 + 1 - core) * FEATS + half * HALF, HALF)
            out[:, part * HALF : (part + 1) * HALF] = grad[:, pl.ds(at, HALF)].astype(F32)


def send_y_kernel(half, place, grad, got, out):
    dp = place[1]
    core, y = lax.rem(dp, 2), lax.div(dp, 2)
    at = pl.multiple_of(((1 - y) * 2 + core) * FEATS + half * HALF, HALF)
    out[...] = grad[:, pl.ds(at, HALF)].astype(F32) + got[...]


def update_kernel(half, place, grad, got, got_y, weight, first, second, *refs):
    out = refs[-1]
    dp = place[1]
    at = pl.multiple_of(dp * FEATS + half * HALF, HALF)
    total = grad[:, pl.ds(at, HALF)].astype(F32) + got[...] + got_y[...]
    new_first = first_decay * first[...] + (1.0 - first_decay) * total
    new_second = second_decay * second[...] + (1.0 - second_decay) * total * total
    first_hat = new_first / (1.0 - first_decay**STEP)
    second_hat = new_second / (1.0 - second_decay**STEP)
    old = weight[...]
    new_weight = old - learning_rate * (
        first_hat / (jnp.sqrt(second_hat) + epsilon) + weight_decay * old
    )
    out[:, 0:HALF] = new_weight
    out[:, HALF : 2 * HALF] = new_first
    out[:, 2 * HALF : 3 * HALF] = new_second


def index_kernel(place, dev, dev_row, col, wanted, codes):
    shard = place[0]
    plane, me = lax.div(shard, PLANE), lax.rem(shard, PLANE)
    d = dev[...]
    r = dev_row[...]
    earlier = lax.broadcasted_iota(I32, (FINE, FINE), 1) < lax.broadcasted_iota(
        I32, (FINE, FINE), 0
    )
    slot = jnp.sum(jnp.where(earlier & (d == r), 1, 0), axis=1, keepdims=True)
    source_xy, source_z = d & (PLANE - 1), d >> 3
    row_of = ((r & (PLANE - 1)) << 3) + (r >> 3)
    left = jnp.where(lax.broadcasted_iota(I32, (64, FINE), 0) == row_of, 1.0, 0.0).astype(BF16)
    right = jnp.where(
        lax.broadcasted_iota(I32, (FINE, 128), 1) == me * SLOTS + slot, col[...].astype(F32), 0.0
    ).astype(BF16)
    table = jnp.dot(left, right, preferred_element_type=F32)
    wanted[...] = table.astype(I32).reshape(PLANE, RING, 128)
    away = (source_z - plane + RING) & (RING - 1)
    none = -1

    def place_in(offsets):
        at = jnp.full((FINE, 1), none, I32)
        for k, offset in offsets:
            at = jnp.where(away == k, source_xy * 64 + offset + slot, at)
        return at

    groups = (
        place_in(((0, 0), (7, 32), (1, 48))),
        place_in(((6, 32), (2, 48))),
        place_in(((5, 32), (3, 48))),
        place_in(((4, 0),)),
        place_in(((0, 16),)),
        place_in(((7, 0), (1, 16))),
        place_in(((6, 0), (2, 16))),
        place_in(((5, 0), (3, 16))),
    )
    lane = lax.broadcasted_iota(I32, (FINE, 128), 1)
    out = jnp.full((FINE, 128), none, I32)
    for g, at in enumerate(groups):
        out = jnp.where(lane == g, at, out)
    codes[...] = out


def asked_rows(asked, plane):
    table = jnp.sum(asked[...], axis=0)
    here = lax.broadcasted_iota(I32, (RING, 128), 0) == plane
    return jnp.sum(jnp.where(here, table, 0), axis=0, keepdims=True)


def pick_from(asked, plane, values):
    rows = values.shape[0]
    chosen = jnp.where(
        lax.broadcasted_iota(I32, (rows, 128), 0) == asked_rows(asked, plane), 1.0, 0.0
    ).astype(BF16)
    return split_dot(chosen, values, ((0,), (0,)))


def pick_kernel(parts, place, asked, *refs):
    out = refs[-1]
    plane = lax.div(place[0], PLANE)
    n = 0
    for away, row, pieces in parts:
        values = refs[n][...]
        if pieces == 2:
            values = jnp.concatenate([values, refs[n + 1][...]], axis=0)
        n += pieces
        got = pick_from(asked, (plane + away + RING) & (RING - 1), values)
        for d in range(PLANE):
            out[d, row : row + SLOTS, :] = got[d * SLOTS : (d + 1) * SLOTS]


def token_kernel(*refs):
    refs[-1][...] = jnp.zeros((8, 128), F32)


def token(arrays):
    return call(
        token_kernel,
        shape(8, 128),
        in_specs=[pl.BlockSpec(memory_space=pl.ANY)] * len(arrays),
        flops=10**10,
    )(*arrays)


def far_dot(at, far):
    rows = far.shape[0] * far.shape[1]
    chosen = jnp.where(
        lax.broadcasted_iota(I32, (FINE, rows), 1) == at, 1.0 - own_share, 0.0
    ).astype(BF16)
    return split_dot(chosen, far.reshape(rows, far.shape[2]))


def far_part(at, far, low, high):
    xy, row = at >> 6, at & 63
    here = (at >= 0) & (row >= low) & (row < high)
    at = jnp.where(here, xy * (high - low) + row - low, -1)
    return far_dot(at, far[:, low:high, :])


def gather_kernel(parts, codes, near, *refs):
    own = lax.broadcasted_iota(I32, (FINE, ROWS), 0) >> 1
    chosen = jnp.where(
        lax.broadcasted_iota(I32, (FINE, ROWS), 1) == own, own_share, 0.0
    ).astype(BF16)
    total = split_dot(chosen, near[...])
    for lane, exchange, low, high in parts:
        total = total + far_part(codes[:, lane : lane + 1], refs[exchange], low, high)
    refs[-1][...] = total


def final_kernel(codes, *refs):
    lane = lax.broadcasted_iota(I32, (FINE, 128), 1) >> 1
    first_half = pl.program_id(0) < 2
    at = codes[:, 3:4]
    for state in range(3):
        acc0, acc1, far, out = (refs[3 * k + state] for k in range(4))
        acc = jnp.where(first_half, acc0[...], acc1[...])
        rows = jnp.where(first_half, far[:, 0:16, :], far[:, 16:32, :])
        mixed = acc + far_part(at, rows, 0, 16)
        out[:, 0:128] = jnp.take_along_axis(mixed, lane, axis=1)
        out[:, 128:256] = jnp.take_along_axis(mixed, lane + 64, axis=1)


PLANES = [[z * PLANE + p for p in range(PLANE)] for z in range(RING)]
UP = [(z * PLANE + p, ((z + 1) % RING) * PLANE + p) for z in range(RING) for p in range(PLANE)]
DOWN = [(b, a) for a, b in UP]
CORE = [(0, 1), (1, 0), (2, 3), (3, 2)]
NEXT_Y = [(0, 2), (2, 0), (1, 3), (3, 1)]


def on_device(grad_parts, weight, first, second, partner_device, partner_column):
    place = jnp.stack([lax.axis_index("shard"), lax.axis_index("dp")]).astype(I32)
    grad = grad_parts[0]

    wanted, codes = call(
        index_kernel,
        (shape(PLANE, RING, 128, dtype=I32), shape(FINE, 128, dtype=I32)),
        in_specs=[scalar(), whole(), whole(), whole()],
        moved=1 << 20,
    )(
        place,
        partner_device,
        partner_device.reshape(1, FINE),
        partner_column.reshape(FINE, 1),
    )
    asked = lax.all_to_all(
        wanted, "shard", split_axis=0, concat_axis=0, axis_index_groups=PLANES, tiled=True
    )

    sends = call(
        send_core_kernel,
        (shape(ROWS, 2 * HALF),) * 2,
        in_specs=[scalar(), whole()],
        moved=3 << 20,
    )(place, grad)
    got_core = [lax.ppermute(s, "dp", CORE) for s in sends]
    state = []
    for half in range(2):
        got = got_core[half]
        passed = call(
            lambda *refs, half=half: send_y_kernel(half, *refs),
            shape(ROWS, HALF),
            grid=(1,),
            in_specs=[
                scalar(),
                pl.BlockSpec((ROWS, 4 * FEATS), lambda i: (0, 0)),
                pl.BlockSpec((ROWS, HALF), lambda i: (0, 0)),
            ],
            out_specs=pl.BlockSpec((ROWS, HALF), lambda i: (0, 0)),
            moved=1 << 20,
        )(place, grad, got)
        got_y = lax.ppermute(passed, "dp", NEXT_Y)
        block = pl.BlockSpec((ROWS, HALF), lambda i, half=half: (0, half))
        state.append(
            call(
                lambda *refs, half=half: update_kernel(half, *refs),
                shape(ROWS, WIDE),
                grid=(1,),
                in_specs=[
                    scalar(),
                    pl.BlockSpec((ROWS, 4 * FEATS), lambda i: (0, 0)),
                    pl.BlockSpec((ROWS, HALF), lambda i: (0, 1)),
                    pl.BlockSpec((ROWS, HALF), lambda i: (0, 0)),
                    block,
                    block,
                    block,
                ]
                + [pl.BlockSpec(memory_space=pl.ANY)] * half,
                out_specs=pl.BlockSpec((ROWS, WIDE), lambda i: (0, 0)),
                moved=2 << 20,
            )(place, grad, got, got_y, weight, first, second, *[asked] * half)
        )

    def pick(parts, sources, after=()):
        return call(
            lambda *refs: pick_kernel(parts, *refs),
            shape(PLANE, SLOTS * len(parts), WIDE),
            in_specs=[scalar()]
            + [whole()] * (1 + len(sources))
            + [pl.BlockSpec(memory_space=pl.ANY)] * len(after),
            flops=len(parts) * SLOTS * PLANE * ROWS * WIDE * 4,
            moved=(len(sources) + 2) << 20,
        )(place, asked, *sources, *after)

    def to_plane(rows):
        return lax.all_to_all(
            rows, "shard", split_axis=0, concat_axis=0, axis_index_groups=PLANES, tiled=True
        )

    def around(pair):
        return lax.ppermute(pair[0], "shard", UP), lax.ppermute(pair[1], "shard", DOWN)

    one = [around((x, x)) for x in state]
    two = [around(pair) for pair in one]
    three = [around(pair) for pair in two]
    far1 = to_plane(pick(((0, 0, 1), (0, 16, 1), (-1, 32, 1), (1, 48, 1)), (*state, *one[0])))
    far2 = to_plane(
        pick(((-1, 0, 1), (1, 16, 1), (-2, 32, 1), (2, 48, 1)), (*one[1], *two[0]), (far1, token((*one[1], *two[0]))))
    )
    far3 = to_plane(
        pick(((-2, 0, 1), (2, 16, 1), (-3, 32, 1), (3, 48, 1)), (*two[1], *three[0]), (far2, token((*two[1], *three[0]))))
    )
    middle = ROWS // 2
    four = [around((pair[0][:middle], pair[1][middle:])) for pair in three]
    far4 = to_plane(pick(((-3, 0, 1), (3, 16, 1)), three[1], (far3, token(three[1]))))
    far5 = to_plane(pick(((4, 0, 2), (4, 16, 2)), (*four[0], *four[1]), (far4, token((*four[0], *four[1])))))

    acc = []
    for half, (parts, far) in enumerate(
        (
            (((0, 0, 0, 16), (0, 0, 32, 64), (1, 1, 32, 64), (2, 2, 32, 64)), (far1, far2, far3)),
            (
                ((4, 0, 16, 32), (5, 1, 0, 32), (6, 2, 0, 32), (7, 3, 0, 32)),
                (far1, far2, far3, far4),
            ),
        )
    ):
        acc.append(
            call(
                lambda *refs, parts=parts: gather_kernel(parts, *refs),
                shape(FINE, WIDE),
                grid=(3,),
                in_specs=[
                    pl.BlockSpec((FINE, 128), lambda i: (0, 0)),
                    pl.BlockSpec((ROWS, HALF), lambda i: (0, i)),
                ]
                + [pl.BlockSpec((PLANE, a.shape[1], HALF), lambda i: (0, 0, i)) for a in far],
                out_specs=pl.BlockSpec((FINE, HALF), lambda i: (0, i)),
                flops=FINE * 1120 * WIDE * 4,
                moved=8 << 20,
            )(codes, state[half], *far)
        )

    def acc_block(half, state):
        def index(j):
            k = jnp.minimum(j, 1) if half == 0 else jnp.maximum(j - 2, 0)
            return 0, state * 2 + k

        return pl.BlockSpec((FINE, 128), index)

    def far_block(state):
        return pl.BlockSpec((PLANE, 32, 128), lambda j: (0, 0, state * 2 + lax.rem(j, 2)))

    return call(
        final_kernel,
        (shape(FINE, 2 * FEATS),) * 3,
        grid=(4,),
        in_specs=[pl.BlockSpec((FINE, 128), lambda j: (0, 0))]
        + [acc_block(half, s) for half in range(2) for s in range(3)]
        + [far_block(s) for s in range(3)],
        out_specs=(pl.BlockSpec((FINE, 256), lambda j: (0, j)),) * 3,
        flops=FINE * 512 * 1536 * 4,
        moved=12 << 20,
    )(codes, acc[0], acc[0], acc[0], acc[1], acc[1], acc[1], far5, far5, far5)


def solution(mesh):
    placed = (
        P("dp", "shard", None),
        P("shard", "dp"),
        P("shard", "dp"),
        P("shard", "dp"),
        P("shard", None),
        P("shard"),
    )
    return jax.shard_map(
        on_device,
        mesh=mesh,
        in_specs=placed,
        out_specs=(P("shard", "dp"), P("shard", "dp"), P("shard", "dp")),
        check_vma=False,
    )
```

```python
import jax
import jax.numpy as jnp
from jax import lax
from jax.experimental import pallas as pl
from jax.experimental.pallas import tpu as pltpu
from jax.sharding import PartitionSpec as P

STEP = 20

first_decay = 0.9
second_decay = 0.95
learning_rate = 0.02
weight_decay = 0.1
epsilon = 1e-08
own_share = 0.75

F32 = jnp.float32
BF16 = jnp.bfloat16
I32 = jnp.int32

ROWS = 224
FINE = 448
FEATS = 512
HALF = 256
WIDE = 3 * HALF
SLOTS = 16
USED = 14
SENT = 4 * USED
PLANE = 8
RING = 8

VMEM = pltpu.CompilerParams(vmem_limit_bytes=12 * 1024 * 1024)


def call(kernel, out, *, grid=None, in_specs=None, out_specs=None, flops=0, moved=0, aliases=None):
    extra = {}
    if grid is not None:
        extra = dict(grid=grid, in_specs=in_specs, out_specs=out_specs)
    elif in_specs is not None:
        extra = dict(in_specs=in_specs)
    return pl.pallas_call(
        kernel,
        out_shape=out,
        compiler_params=VMEM,
        input_output_aliases=aliases or {},
        cost_estimate=pl.CostEstimate(flops=flops, bytes_accessed=moved, transcendentals=0),
        **extra,
    )


def shape(*dims, dtype=F32):
    return jax.ShapeDtypeStruct(dims, dtype)


def whole():
    return pl.BlockSpec(memory_space=pltpu.VMEM)


def scalar():
    return pl.BlockSpec(memory_space=pltpu.SMEM)


def split_dot(chosen, values, contract=((1,), (0,))):
    high = values.astype(BF16)
    low = (values - high.astype(F32)).astype(BF16)
    dims = (contract, ((), ()))
    return lax.dot_general(chosen, high, dims, preferred_element_type=F32) + lax.dot_general(
        chosen, low, dims, preferred_element_type=F32
    )


def send_core_kernel(place, grad, out0, out1):
    dp = place[1]
    core, y = lax.rem(dp, 2), lax.div(dp, 2)
    for half, out in enumerate((out0, out1)):
        for part, row in enumerate((1 - y, y)):
            at = pl.multiple_of((row * 2 + 1 - core) * FEATS + half * HALF, HALF)
            out[:, part * HALF : (part + 1) * HALF] = grad[:, pl.ds(at, HALF)].astype(F32)


def send_y_kernel(half, place, grad, got, out):
    dp = place[1]
    core, y = lax.rem(dp, 2), lax.div(dp, 2)
    at = pl.multiple_of(((1 - y) * 2 + core) * FEATS + half * HALF, HALF)
    out[...] = grad[:, pl.ds(at, HALF)].astype(F32) + got[...]


def update_kernel(half, place, grad, got, got_y, weight, first, second, out):
    dp = place[1]
    at = pl.multiple_of(dp * FEATS + half * HALF, HALF)
    total = grad[:, pl.ds(at, HALF)].astype(F32) + got[...] + got_y[...]
    new_first = first_decay * first[...] + (1.0 - first_decay) * total
    new_second = second_decay * second[...] + (1.0 - second_decay) * total * total
    first_hat = new_first / (1.0 - first_decay**STEP)
    second_hat = new_second / (1.0 - second_decay**STEP)
    old = weight[...]
    new_weight = old - learning_rate * (
        first_hat / (jnp.sqrt(second_hat) + epsilon) + weight_decay * old
    )
    out[:, 0:HALF] = new_weight
    out[:, HALF : 2 * HALF] = new_first
    out[:, 2 * HALF : 3 * HALF] = new_second


def index_kernel(place, dev, dev_row, col, wanted, codes):
    shard = place[0]
    plane, me = lax.div(shard, PLANE), lax.rem(shard, PLANE)
    d = dev[...]
    r = dev_row[...]
    earlier = lax.broadcasted_iota(I32, (FINE, FINE), 1) < lax.broadcasted_iota(
        I32, (FINE, FINE), 0
    )
    slot = jnp.sum(jnp.where(earlier & (d == r), 1, 0), axis=1, keepdims=True)
    source_xy, source_z = d & (PLANE - 1), d >> 3
    row_of = ((r & (PLANE - 1)) << 3) + (r >> 3)
    left = jnp.where(lax.broadcasted_iota(I32, (64, FINE), 0) == row_of, 1.0, 0.0).astype(BF16)
    right = jnp.where(
        lax.broadcasted_iota(I32, (FINE, 128), 1) == me * SLOTS + slot, col[...].astype(F32), 0.0
    ).astype(BF16)
    table = jnp.dot(left, right, preferred_element_type=F32)
    wanted[...] = table.astype(I32).reshape(PLANE, RING, 128)
    away = (source_z - plane + RING) & (RING - 1)
    none = -1

    def place_in(offsets):
        at = jnp.full((FINE, 1), none, I32)
        for k, offset in offsets:
            at = jnp.where(away == k, source_xy * 128 + offset + slot, at)
        return at

    groups = (
        place_in(((0, 0), (7, 28), (1, 42))),
        place_in(((6, 28), (2, 42))),
        place_in(((5, 28), (3, 42))),
        place_in(((4, 28),)),
        place_in(((0, 14),)),
        place_in(((7, 0), (1, 14))),
        place_in(((6, 0), (2, 14))),
        place_in(((5, 0), (3, 14), (4, 42))),
    )
    lane = lax.broadcasted_iota(I32, (FINE, 128), 1)
    out = jnp.full((FINE, 128), none, I32)
    for g, at in enumerate(groups):
        out = jnp.where(lane == g, at, out)
    codes[...] = out


def asked_rows(asked, plane):
    here = lax.broadcasted_iota(I32, (RING, 128), 0) == plane
    return jnp.sum(jnp.where(here, asked[...], 0), axis=0, keepdims=True)


def pick_from(asked, plane, values):
    rows = values.shape[0]
    chosen = jnp.where(
        lax.broadcasted_iota(I32, (rows, 128), 0) == asked_rows(asked, plane), 1.0, 0.0
    ).astype(BF16)
    return split_dot(chosen, values, ((0,), (0,)))


def pick_kernel(planes, place, asked, *refs):
    out = refs[-1]
    plane = lax.div(place[0], PLANE)
    for n, away in enumerate(planes):
        got = pick_from(asked, (plane + away + RING) & (RING - 1), refs[n][...])
        for d in range(PLANE):
            out[d, n * USED : (n + 1) * USED, :] = got[d * SLOTS : d * SLOTS + USED]


def held_kernel(*refs):
    pass


def hold(arrays, *until):
    n = len(arrays)
    return pl.pallas_call(
        held_kernel,
        out_shape=tuple(shape(*a.shape) for a in arrays),
        in_specs=[pl.BlockSpec(memory_space=pl.ANY)] * (n + len(until)),
        out_specs=(pl.BlockSpec(memory_space=pl.ANY),) * n,
        input_output_aliases={i: i for i in range(n)},
    )(*arrays, *until)


def token_kernel(*refs):
    refs[-1][...] = jnp.zeros((8, 128), F32)


def token(arrays):
    return call(
        token_kernel,
        shape(8, 128),
        in_specs=[pl.BlockSpec(memory_space=pl.ANY)] * len(arrays),
        flops=10**10,
    )(*arrays)


def far_dot(at, far):
    rows = far.shape[0] * far.shape[1]
    chosen = jnp.where(
        lax.broadcasted_iota(I32, (FINE, rows), 1) == at, 1.0 - own_share, 0.0
    ).astype(BF16)
    return split_dot(chosen, far.reshape(rows, far.shape[2]))


def far_part(codes, lane, far, low, high):
    at = codes[:, lane : lane + 1]
    xy, row = at >> 7, at & 127
    here = (at >= 0) & (row >= low) & (row < high)
    at = jnp.where(here, xy * (high - low) + row - low, -1)
    return far_dot(at, far[:, low:high, :])


def near_part(near):
    own = lax.broadcasted_iota(I32, (FINE, ROWS), 0) >> 1
    chosen = jnp.where(
        lax.broadcasted_iota(I32, (FINE, ROWS), 1) == own, own_share, 0.0
    ).astype(BF16)
    return split_dot(chosen, near[...])


def gather_kernel(parts, codes, near, *refs):
    total = near_part(near)
    for lane, exchange, low, high in parts:
        total = total + far_part(codes, lane, refs[exchange], low, high)
    refs[-1][...] = total


def doubled(values):
    row = lax.broadcasted_iota(I32, (128, 256), 0)
    lane = lax.broadcasted_iota(I32, (128, 256), 1) >> 1
    twice = jnp.where(row == lane, 1.0, 0.0).astype(BF16)
    high = values.astype(BF16)
    low = (values - high.astype(F32)).astype(BF16)
    return jnp.dot(high, twice, preferred_element_type=F32) + jnp.dot(
        low, twice, preferred_element_type=F32
    )


def final_kernel(codes, *refs):
    first_half = pl.program_id(0) < 2
    at = jnp.where(first_half, codes[:, 3:4], codes[:, 7:8])
    at = jnp.where(at >= 0, (at >> 7) * SENT + (at & 127), -1)
    for state in range(3):
        acc0, acc1, far, out = (refs[3 * k + state] for k in range(4))
        acc = jnp.where(first_half, acc0[...], acc1[...])
        out[...] = doubled(acc + far_dot(at, far[...]))


PLANES = [[z * PLANE + p for p in range(PLANE)] for z in range(RING)]
UP = [(z * PLANE + p, ((z + 1) % RING) * PLANE + p) for z in range(RING) for p in range(PLANE)]
DOWN = [(b, a) for a, b in UP]
CORE = [(0, 1), (1, 0), (2, 3), (3, 2)]
NEXT_Y = [(0, 2), (2, 0), (1, 3), (3, 1)]


def on_device(grad_parts, weight, first, second, partner_device, partner_column):
    place = jnp.stack([lax.axis_index("shard"), lax.axis_index("dp")]).astype(I32)
    grad = grad_parts[0]

    wanted, codes = call(
        index_kernel,
        (shape(PLANE, RING, 128, dtype=I32), shape(FINE, 128, dtype=I32)),
        in_specs=[scalar(), whole(), whole(), whole()],
        moved=1 << 20,
    )(
        place,
        partner_device,
        partner_device.reshape(1, FINE),
        partner_column.reshape(FINE, 1),
    )
    asked = jnp.sum(
        lax.all_to_all(
            wanted, "shard", split_axis=0, concat_axis=0, axis_index_groups=PLANES, tiled=True
        ),
        axis=0,
    )
    sends = call(
        send_core_kernel,
        (shape(ROWS, 2 * HALF),) * 2,
        in_specs=[scalar(), whole()],
        moved=3 << 20,
    )(place, grad)
    got_core = [lax.ppermute(s, "dp", CORE) for s in sends]
    state = []
    for half in range(2):
        got = got_core[half]
        passed = call(
            lambda *refs, half=half: send_y_kernel(half, *refs),
            shape(ROWS, HALF),
            grid=(1,),
            in_specs=[
                scalar(),
                pl.BlockSpec((ROWS, 4 * FEATS), lambda i: (0, 0)),
                pl.BlockSpec((ROWS, HALF), lambda i: (0, 0)),
            ],
            out_specs=pl.BlockSpec((ROWS, HALF), lambda i: (0, 0)),
            moved=1 << 20,
        )(place, grad, got)
        got_y = lax.ppermute(passed, "dp", NEXT_Y)
        block = pl.BlockSpec((ROWS, HALF), lambda i, half=half: (0, half))
        state.append(
            call(
                lambda *refs, half=half: update_kernel(half, *refs),
                shape(ROWS, WIDE),
                grid=(1,),
                in_specs=[
                    scalar(),
                    pl.BlockSpec((ROWS, 4 * FEATS), lambda i: (0, 0)),
                    pl.BlockSpec((ROWS, HALF), lambda i: (0, 1)),
                    pl.BlockSpec((ROWS, HALF), lambda i: (0, 0)),
                    block,
                    block,
                    block,
                ],
                out_specs=pl.BlockSpec((ROWS, WIDE), lambda i: (0, 0)),
                moved=2 << 20,
            )(place, grad, got, got_y, weight, first, second)
        )

    def pick(planes, sources, after=()):
        after = (*after, token(sources))
        return call(
            lambda *refs: pick_kernel(planes, *refs),
            shape(PLANE, SENT, WIDE),
            in_specs=[scalar()]
            + [whole()] * (1 + len(sources))
            + [pl.BlockSpec(memory_space=pl.ANY)] * len(after),
            flops=4 * SLOTS * PLANE * ROWS * WIDE * 4,
            moved=5 << 20,
        )(place, asked, *sources, *after)

    def to_plane(rows):
        return lax.all_to_all(
            rows, "shard", split_axis=0, concat_axis=0, axis_index_groups=PLANES, tiled=True
        )

    def around(pair):
        return lax.ppermute(pair[0], "shard", UP), lax.ppermute(pair[1], "shard", DOWN)

    one = [around((x, x)) for x in state]
    one[0] = hold(one[0], asked)
    two = [around(pair) for pair in one]
    three = [around(pair) for pair in two]
    four = (
        lax.ppermute(three[0][0], "shard", UP),
        lax.ppermute(three[1][1], "shard", DOWN),
    )
    far1 = to_plane(pick((0, 0, -1, 1), (*state, *one[0])))
    far2 = to_plane(pick((-1, 1, -2, 2), (*one[1], *two[0]), (far1,)))
    far3 = to_plane(pick((-2, 2, -3, 3), (*two[1], *three[0]), (far2,)))
    far4 = to_plane(pick((-3, 3, 4, 4), (*three[1], *four), (far3,)))

    acc = []
    for half, parts in enumerate(
        (
            ((0, 0, 0, 56), (1, 1, 24, 56), (2, 2, 24, 56)),
            ((4, 0, 8, 32), (5, 1, 0, 32), (6, 2, 0, 32)),
        )
    ):
        acc.append(
            call(
                lambda *refs, parts=parts: gather_kernel(parts, *refs),
                shape(FINE, WIDE),
                grid=(3,),
                in_specs=[
                    pl.BlockSpec((FINE, 128), lambda i: (0, 0)),
                    pl.BlockSpec((ROWS, HALF), lambda i: (0, i)),
                ]
                + [pl.BlockSpec((PLANE, SENT, HALF), lambda i: (0, 0, i))] * 3,
                out_specs=pl.BlockSpec((FINE, HALF), lambda i: (0, i)),
                flops=FINE * 1120 * WIDE * 4,
                moved=8 << 20,
            )(codes, state[half], far1, far2, far3)
        )

    def acc_block(half, state):
        def index(j):
            k = jnp.minimum(j, 1) if half == 0 else jnp.maximum(j - 2, 0)
            return 0, state * 2 + k

        return pl.BlockSpec((FINE, 128), index)

    def far_block(state):
        return pl.BlockSpec((PLANE, SENT, 128), lambda j: (0, 0, state * 2 + lax.rem(j, 2)))

    return call(
        final_kernel,
        (shape(FINE, 2 * FEATS),) * 3,
        grid=(4,),
        in_specs=[pl.BlockSpec((FINE, 128), lambda j: (0, 0))]
        + [acc_block(half, s) for half in range(2) for s in range(3)]
        + [far_block(s) for s in range(3)],
        out_specs=(pl.BlockSpec((FINE, 256), lambda j: (0, j)),) * 3,
        flops=FINE * 512 * 1536 * 4,
        moved=12 << 20,
    )(codes, acc[0], acc[0], acc[0], acc[1], acc[1], acc[1], far4, far4, far4)


def solution(mesh):
    placed = (
        P("dp", "shard", None),
        P("shard", "dp"),
        P("shard", "dp"),
        P("shard", "dp"),
        P("shard", None),
        P("shard"),
    )
    return jax.shard_map(
        on_device,
        mesh=mesh,
        in_specs=placed,
        out_specs=(P("shard", "dp"), P("shard", "dp"), P("shard", "dp")),
        check_vma=False,
    )
```

```python
import jax
import jax.numpy as jnp
from jax import lax
from jax.experimental import pallas as pl
from jax.experimental.pallas import tpu as pltpu
from jax.sharding import PartitionSpec as P

STEP = 20

first_decay = 0.9
second_decay = 0.95
learning_rate = 0.02
weight_decay = 0.1
epsilon = 1e-08
own_share = 0.75

F32 = jnp.float32
BF16 = jnp.bfloat16
I32 = jnp.int32

ROWS = 224
FINE = 448
FEATS = 512
HALF = 256
WIDE = 3 * HALF
SLOTS = 16
USED = 14
SENT = 4 * USED
PLANE = 8
RING = 8

VMEM = pltpu.CompilerParams(vmem_limit_bytes=12 * 1024 * 1024)


def call(kernel, out, *, grid=None, in_specs=None, out_specs=None, flops=0, moved=0, aliases=None):
    extra = {}
    if grid is not None:
        extra = dict(grid=grid, in_specs=in_specs, out_specs=out_specs)
    elif in_specs is not None:
        extra = dict(in_specs=in_specs)
    return pl.pallas_call(
        kernel,
        out_shape=out,
        compiler_params=VMEM,
        input_output_aliases=aliases or {},
        cost_estimate=pl.CostEstimate(flops=flops, bytes_accessed=moved, transcendentals=0),
        **extra,
    )


def shape(*dims, dtype=F32):
    return jax.ShapeDtypeStruct(dims, dtype)


def whole():
    return pl.BlockSpec(memory_space=pltpu.VMEM)


def scalar():
    return pl.BlockSpec(memory_space=pltpu.SMEM)


def halves(values):
    high = values.astype(BF16)
    return high, (values - high.astype(F32)).astype(BF16)


def split_dot(chosen, values, contract=((1,), (0,))):
    dims = (contract, ((), ()))
    high, low = halves(values)
    return lax.dot_general(chosen, high, dims, preferred_element_type=F32) + lax.dot_general(
        chosen, low, dims, preferred_element_type=F32
    )


def send_core_kernel(place, grad, out0, out1):
    dp = place[1]
    core, y = lax.rem(dp, 2), lax.div(dp, 2)
    for half, out in enumerate((out0, out1)):
        for part, row in enumerate((1 - y, y)):
            at = pl.multiple_of((row * 2 + 1 - core) * FEATS + half * HALF, HALF)
            out[:, part * HALF : (part + 1) * HALF] = grad[:, pl.ds(at, HALF)].astype(F32)


def send_y_kernel(half, place, grad, got, out):
    dp = place[1]
    core, y = lax.rem(dp, 2), lax.div(dp, 2)
    at = pl.multiple_of(((1 - y) * 2 + core) * FEATS + half * HALF, HALF)
    out[...] = grad[:, pl.ds(at, HALF)].astype(F32) + got[...]


def update_kernel(half, place, grad, got, got_y, weight, first, second, *refs):
    out = refs[-1]
    dp = place[1]
    at = pl.multiple_of(dp * FEATS + half * HALF, HALF)
    total = grad[:, pl.ds(at, HALF)].astype(F32) + got[...] + got_y[...]
    new_first = first_decay * first[...] + (1.0 - first_decay) * total
    new_second = second_decay * second[...] + (1.0 - second_decay) * total * total
    first_hat = new_first / (1.0 - first_decay**STEP)
    second_hat = new_second / (1.0 - second_decay**STEP)
    old = weight[...]
    new_weight = old - learning_rate * (
        first_hat / (jnp.sqrt(second_hat) + epsilon) + weight_decay * old
    )
    out[:, 0:HALF] = new_weight
    out[:, HALF : 2 * HALF] = new_first
    out[:, 2 * HALF : 3 * HALF] = new_second


def index_kernel(place, dev, dev_row, col, wanted, codes):
    shard = place[0]
    plane, me = lax.div(shard, PLANE), lax.rem(shard, PLANE)
    d = dev[...]
    r = dev_row[...]
    earlier = lax.broadcasted_iota(I32, (FINE, FINE), 1) < lax.broadcasted_iota(
        I32, (FINE, FINE), 0
    )
    slot = jnp.sum(jnp.where(earlier & (d == r), 1, 0), axis=1, keepdims=True)
    source_xy, source_z = d & (PLANE - 1), d >> 3
    row_of = ((r & (PLANE - 1)) << 3) + (r >> 3)
    left = jnp.where(lax.broadcasted_iota(I32, (64, FINE), 0) == row_of, 1.0, 0.0).astype(BF16)
    right = jnp.where(
        lax.broadcasted_iota(I32, (FINE, 128), 1) == me * SLOTS + slot, col[...].astype(F32), 0.0
    ).astype(BF16)
    table = jnp.dot(left, right, preferred_element_type=F32)
    wanted[...] = table.astype(I32).reshape(PLANE, RING, 128)
    away = (source_z - plane + RING) & (RING - 1)
    none = -1

    def place_in(offsets):
        at = jnp.full((FINE, 1), none, I32)
        for k, offset in offsets:
            at = jnp.where(away == k, source_xy * 128 + offset + slot, at)
        return at

    groups = (
        place_in(((0, 0), (7, 28), (1, 42))),
        place_in(((6, 28), (2, 42))),
        place_in(((5, 28), (3, 42))),
        place_in(((4, 28),)),
        place_in(((0, 14),)),
        place_in(((7, 0), (1, 14))),
        place_in(((6, 0), (2, 14))),
        place_in(((5, 0), (3, 14), (4, 42))),
    )
    lane = lax.broadcasted_iota(I32, (FINE, 128), 1)
    out = jnp.full((FINE, 128), none, I32)
    for g, at in enumerate(groups):
        out = jnp.where(lane == g, at, out)
    codes[...] = out


def asked_rows(asked, plane):
    here = lax.broadcasted_iota(I32, (RING, 128), 0) == plane
    return jnp.sum(jnp.where(here, asked[...], 0), axis=0, keepdims=True)


def pick_from(asked, plane, values):
    rows = values.shape[0]
    chosen = jnp.where(
        lax.broadcasted_iota(I32, (rows, 128), 0) == asked_rows(asked, plane), 1.0, 0.0
    ).astype(BF16)
    return split_dot(chosen, values, ((0,), (0,)))


def pick_kernel(planes, place, asked, *refs):
    out = refs[-1]
    plane = lax.div(place[0], PLANE)
    for n, away in enumerate(planes):
        got = pick_from(asked, (plane + away + RING) & (RING - 1), refs[n][...])
        for d in range(PLANE):
            out[d, n * USED : (n + 1) * USED, :] = got[d * SLOTS : d * SLOTS + USED]


def held_kernel(*refs):
    pass


def hold(arrays, *until):
    n = len(arrays)
    return pl.pallas_call(
        held_kernel,
        out_shape=tuple(shape(*a.shape) for a in arrays),
        in_specs=[pl.BlockSpec(memory_space=pl.ANY)] * (n + len(until)),
        out_specs=(pl.BlockSpec(memory_space=pl.ANY),) * n,
        input_output_aliases={i: i for i in range(n)},
    )(*arrays, *until)


def token_kernel(*refs):
    refs[-1][...] = jnp.zeros((8, 128), F32)


def token(arrays):
    return call(
        token_kernel,
        shape(8, 128),
        in_specs=[pl.BlockSpec(memory_space=pl.ANY)] * len(arrays),
        flops=10**10,
    )(*arrays)


def far_dot(at, far):
    rows = far.shape[0] * far.shape[1]
    chosen = jnp.where(
        lax.broadcasted_iota(I32, (FINE, rows), 1) == at, 1.0 - own_share, 0.0
    ).astype(BF16)
    return split_dot(chosen, far.reshape(rows, far.shape[2]))


def far_part(codes, lane, far, low, high):
    at = codes[:, lane : lane + 1]
    xy, row = at >> 7, at & 127
    here = (at >= 0) & (row >= low) & (row < high)
    at = jnp.where(here, xy * (high - low) + row - low, -1)
    return far_dot(at, far[:, low:high, :])


def near_part(near):
    own = lax.broadcasted_iota(I32, (FINE, ROWS), 0) >> 1
    chosen = jnp.where(
        lax.broadcasted_iota(I32, (FINE, ROWS), 1) == own, own_share, 0.0
    ).astype(BF16)
    return split_dot(chosen, near[...])


def gather_kernel(parts, codes, near, *refs):
    total = near_part(near)
    for lane, exchange, low, high in parts:
        total = total + far_part(codes, lane, refs[exchange], low, high)
    refs[-1][...] = total


def final_kernel(codes, *refs):
    first_half = pl.program_id(0) < 2
    at = jnp.where(first_half, codes[:, 3:4], codes[:, 7:8])
    at = jnp.where(at >= 0, (at >> 7) * SENT + (at & 127), -1)
    rows = PLANE * SENT
    chosen = jnp.where(
        lax.broadcasted_iota(I32, (FINE, rows), 1) == at, 1.0 - own_share, 0.0
    ).astype(BF16)
    row = lax.broadcasted_iota(I32, (256, 256), 0) & 127
    lane = lax.broadcasted_iota(I32, (256, 256), 1) >> 1
    twice = jnp.where(row == lane, 1.0, 0.0).astype(BF16)
    far = [piece for k in range(3) for piece in halves(refs[6 + k][...].reshape(rows, 128))]
    far = jnp.dot(chosen, jnp.concatenate(far, axis=1), preferred_element_type=F32)
    for state in range(3):
        acc0, acc1, out = (refs[3 * k + state] for k in (0, 1, 3))
        at = state * 256
        mixed = jnp.where(first_half, acc0[...], acc1[...])
        mixed = mixed + far[:, at : at + 128] + far[:, at + 128 : at + 256]
        out[...] = jnp.dot(
            jnp.concatenate(halves(mixed), axis=1), twice, preferred_element_type=F32
        )


PLANES = [[z * PLANE + p for p in range(PLANE)] for z in range(RING)]
UP = [(z * PLANE + p, ((z + 1) % RING) * PLANE + p) for z in range(RING) for p in range(PLANE)]
DOWN = [(b, a) for a, b in UP]
CORE = [(0, 1), (1, 0), (2, 3), (3, 2)]
NEXT_Y = [(0, 2), (2, 0), (1, 3), (3, 1)]


def on_device(grad_parts, weight, first, second, partner_device, partner_column):
    place = jnp.stack([lax.axis_index("shard"), lax.axis_index("dp")]).astype(I32)
    grad = grad_parts[0]

    wanted, codes = call(
        index_kernel,
        (shape(PLANE, RING, 128, dtype=I32), shape(FINE, 128, dtype=I32)),
        in_specs=[scalar(), whole(), whole(), whole()],
        moved=1 << 20,
    )(
        place,
        partner_device,
        partner_device.reshape(1, FINE),
        partner_column.reshape(FINE, 1),
    )
    asked = jnp.sum(
        lax.all_to_all(
            wanted, "shard", split_axis=0, concat_axis=0, axis_index_groups=PLANES, tiled=True
        ),
        axis=0,
    )
    sends = call(
        send_core_kernel,
        (shape(ROWS, 2 * HALF),) * 2,
        in_specs=[scalar(), whole()],
        moved=3 << 20,
    )(place, grad)
    got_core = [lax.ppermute(s, "dp", CORE) for s in sends]
    state = []
    for half in range(2):
        got = got_core[half]
        passed = call(
            lambda *refs, half=half: send_y_kernel(half, *refs),
            shape(ROWS, HALF),
            grid=(1,),
            in_specs=[
                scalar(),
                pl.BlockSpec((ROWS, 4 * FEATS), lambda i: (0, 0)),
                pl.BlockSpec((ROWS, HALF), lambda i: (0, 0)),
            ],
            out_specs=pl.BlockSpec((ROWS, HALF), lambda i: (0, 0)),
            moved=1 << 20,
        )(place, grad, got)
        got_y = lax.ppermute(passed, "dp", NEXT_Y)
        block = pl.BlockSpec((ROWS, HALF), lambda i, half=half: (0, half))
        state.append(
            call(
                lambda *refs, half=half: update_kernel(half, *refs),
                shape(ROWS, WIDE),
                grid=(1,),
                in_specs=[
                    scalar(),
                    pl.BlockSpec((ROWS, 4 * FEATS), lambda i: (0, 0)),
                    pl.BlockSpec((ROWS, HALF), lambda i: (0, 1)),
                    pl.BlockSpec((ROWS, HALF), lambda i: (0, 0)),
                    block,
                    block,
                    block,
                ]
                + [pl.BlockSpec(memory_space=pl.ANY)] * half,
                out_specs=pl.BlockSpec((ROWS, WIDE), lambda i: (0, 0)),
                moved=2 << 20,
            )(place, grad, got, got_y, weight, first, second, *[wanted] * half)
        )

    def pick(planes, sources, after=()):
        if after:
            after = (*after, token(sources))
        return call(
            lambda *refs: pick_kernel(planes, *refs),
            shape(PLANE, SENT, WIDE),
            in_specs=[scalar()]
            + [whole()] * (1 + len(sources))
            + [pl.BlockSpec(memory_space=pl.ANY)] * len(after),
            flops=4 * SLOTS * PLANE * ROWS * WIDE * 4,
            moved=5 << 20,
        )(place, asked, *sources, *after)

    def to_plane(rows):
        return lax.all_to_all(
            rows, "shard", split_axis=0, concat_axis=0, axis_index_groups=PLANES, tiled=True
        )

    def around(pair):
        return lax.ppermute(pair[0], "shard", UP), lax.ppermute(pair[1], "shard", DOWN)

    one = [around((x, x)) for x in state]
    one[1] = hold(one[1], asked)
    two = [around(pair) for pair in one]
    three = [around(pair) for pair in two]
    four = (
        lax.ppermute(three[0][0], "shard", UP),
        lax.ppermute(three[1][1], "shard", DOWN),
    )
    far1 = to_plane(pick((0, 0, -1, 1), (*state, *one[0])))
    far2 = to_plane(pick((-1, 1, -2, 2), (*one[1], *two[0]), (far1,)))
    far3 = to_plane(pick((-2, 2, -3, 3), (*two[1], *three[0]), (far2,)))
    far4 = to_plane(pick((-3, 3, 4, 4), (*three[1], *four), (far3,)))

    acc = []
    for half, parts in enumerate(
        (
            ((0, 0, 0, 56), (1, 1, 24, 56), (2, 2, 24, 56)),
            ((4, 0, 8, 32), (5, 1, 0, 32), (6, 2, 0, 32)),
        )
    ):
        acc.append(
            call(
                lambda *refs, parts=parts: gather_kernel(parts, *refs),
                shape(FINE, WIDE),
                grid=(3,),
                in_specs=[
                    pl.BlockSpec((FINE, 128), lambda i: (0, 0)),
                    pl.BlockSpec((ROWS, HALF), lambda i: (0, i)),
                ]
                + [pl.BlockSpec((PLANE, SENT, HALF), lambda i: (0, 0, i))] * 3,
                out_specs=pl.BlockSpec((FINE, HALF), lambda i: (0, i)),
                flops=FINE * 1120 * WIDE * 4,
                moved=8 << 20,
            )(codes, state[half], far1, far2, far3)
        )

    def acc_block(half, state):
        def index(j):
            k = jnp.minimum(j, 1) if half == 0 else jnp.maximum(j - 2, 0)
            return 0, state * 2 + k

        return pl.BlockSpec((FINE, 128), index)

    def far_block(state):
        return pl.BlockSpec((PLANE, SENT, 128), lambda j: (0, 0, state * 2 + lax.rem(j, 2)))

    return call(
        final_kernel,
        (shape(FINE, 2 * FEATS),) * 3,
        grid=(4,),
        in_specs=[pl.BlockSpec((FINE, 128), lambda j: (0, 0))]
        + [acc_block(half, s) for half in range(2) for s in range(3)]
        + [far_block(s) for s in range(3)],
        out_specs=(pl.BlockSpec((FINE, 256), lambda j: (0, j)),) * 3,
        flops=FINE * 512 * 1536 * 4,
        moved=12 << 20,
    )(codes, acc[0], acc[0], acc[0], acc[1], acc[1], acc[1], far4, far4, far4)


def solution(mesh):
    placed = (
        P("dp", "shard", None),
        P("shard", "dp"),
        P("shard", "dp"),
        P("shard", "dp"),
        P("shard", None),
        P("shard"),
    )
    return jax.shard_map(
        on_device,
        mesh=mesh,
        in_specs=placed,
        out_specs=(P("shard", "dp"), P("shard", "dp"), P("shard", "dp")),
        check_vma=False,
    )
```

```python
import jax
import jax.numpy as jnp
from jax import lax
from jax.experimental import pallas as pl
from jax.experimental.pallas import tpu as pltpu
from jax.sharding import PartitionSpec as P

STEP = 20

first_decay = 0.9
second_decay = 0.95
learning_rate = 0.02
weight_decay = 0.1
epsilon = 1e-08
own_share = 0.75

F32 = jnp.float32
BF16 = jnp.bfloat16
I32 = jnp.int32

ROWS = 224
FINE = 448
FEATS = 512
HALF = 256
WIDE = 3 * HALF
SLOTS = 16
USED = 14
SENT = 4 * USED
PLANE = 8
RING = 8

VMEM = pltpu.CompilerParams(vmem_limit_bytes=12 * 1024 * 1024)


def call(kernel, out, *, grid=None, in_specs=None, out_specs=None, flops=0, moved=0, aliases=None):
    extra = {}
    if grid is not None:
        extra = dict(grid=grid, in_specs=in_specs, out_specs=out_specs)
    elif in_specs is not None:
        extra = dict(in_specs=in_specs)
    return pl.pallas_call(
        kernel,
        out_shape=out,
        compiler_params=VMEM,
        input_output_aliases=aliases or {},
        cost_estimate=pl.CostEstimate(flops=flops, bytes_accessed=moved, transcendentals=0),
        **extra,
    )


def shape(*dims, dtype=F32):
    return jax.ShapeDtypeStruct(dims, dtype)


def whole():
    return pl.BlockSpec(memory_space=pltpu.VMEM)


def scalar():
    return pl.BlockSpec(memory_space=pltpu.SMEM)


def halves(values):
    high = values.astype(BF16)
    return high, (values - high.astype(F32)).astype(BF16)


def split_dot(chosen, values, contract=((1,), (0,))):
    dims = (contract, ((), ()))
    high, low = halves(values)
    return lax.dot_general(chosen, high, dims, preferred_element_type=F32) + lax.dot_general(
        chosen, low, dims, preferred_element_type=F32
    )


def send_core_kernel(place, grad, out0, out1):
    dp = place[1]
    core, y = lax.rem(dp, 2), lax.div(dp, 2)
    for half, out in enumerate((out0, out1)):
        for part, row in enumerate((1 - y, y)):
            at = pl.multiple_of((row * 2 + 1 - core) * FEATS + half * HALF, HALF)
            out[:, part * HALF : (part + 1) * HALF] = grad[:, pl.ds(at, HALF)].astype(F32)


def send_y_kernel(half, place, grad, got, out):
    dp = place[1]
    core, y = lax.rem(dp, 2), lax.div(dp, 2)
    at = pl.multiple_of(((1 - y) * 2 + core) * FEATS + half * HALF, HALF)
    out[...] = grad[:, pl.ds(at, HALF)].astype(F32) + got[...]


def update_kernel(half, place, grad, got, got_y, weight, first, second, *refs):
    out = refs[-1]
    dp = place[1]
    at = pl.multiple_of(dp * FEATS + half * HALF, HALF)
    total = grad[:, pl.ds(at, HALF)].astype(F32) + got[...] + got_y[...]
    new_first = first_decay * first[...] + (1.0 - first_decay) * total
    new_second = second_decay * second[...] + (1.0 - second_decay) * total * total
    first_hat = new_first / (1.0 - first_decay**STEP)
    second_hat = new_second / (1.0 - second_decay**STEP)
    old = weight[...]
    new_weight = old - learning_rate * (
        first_hat / (jnp.sqrt(second_hat) + epsilon) + weight_decay * old
    )
    out[:, 0:HALF] = new_weight
    out[:, HALF : 2 * HALF] = new_first
    out[:, 2 * HALF : 3 * HALF] = new_second


def index_kernel(place, dev, dev_row, col, wanted, codes):
    shard = place[0]
    plane, me = lax.div(shard, PLANE), lax.rem(shard, PLANE)
    d = dev[...]
    r = dev_row[...]
    earlier = lax.broadcasted_iota(I32, (FINE, FINE), 1) < lax.broadcasted_iota(
        I32, (FINE, FINE), 0
    )
    slot = jnp.sum(jnp.where(earlier & (d == r), 1, 0), axis=1, keepdims=True)
    source_xy, source_z = d & (PLANE - 1), d >> 3
    row_of = ((r & (PLANE - 1)) << 3) + (r >> 3)
    left = jnp.where(lax.broadcasted_iota(I32, (64, FINE), 0) == row_of, 1.0, 0.0).astype(BF16)
    right = jnp.where(
        lax.broadcasted_iota(I32, (FINE, 128), 1) == me * SLOTS + slot, col[...].astype(F32), 0.0
    ).astype(BF16)
    table = jnp.dot(left, right, preferred_element_type=F32)
    wanted[...] = table.astype(I32).reshape(PLANE, RING, 128)
    away = (source_z - plane + RING) & (RING - 1)
    none = -1

    def place_in(offsets):
        at = jnp.full((FINE, 1), none, I32)
        for k, offset in offsets:
            at = jnp.where(away == k, source_xy * 128 + offset + slot, at)
        return at

    groups = (
        place_in(((0, 0), (7, 28), (1, 42))),
        place_in(((6, 28), (2, 42))),
        place_in(((5, 28), (3, 42))),
        place_in(((4, 28),)),
        place_in(((0, 14),)),
        place_in(((7, 0), (1, 14))),
        place_in(((6, 0), (2, 14))),
        place_in(((5, 0), (3, 14), (4, 42))),
    )
    lane = lax.broadcasted_iota(I32, (FINE, 128), 1)
    out = jnp.full((FINE, 128), none, I32)
    for g, at in enumerate(groups):
        out = jnp.where(lane == g, at, out)
    codes[...] = out


def asked_rows(asked, plane):
    here = lax.broadcasted_iota(I32, (RING, 128), 0) == plane
    return jnp.sum(jnp.where(here, jnp.sum(asked[...], axis=0), 0), axis=0, keepdims=True)


def pick_from(asked, plane, values):
    rows = values.shape[0]
    chosen = jnp.where(
        lax.broadcasted_iota(I32, (rows, 128), 0) == asked_rows(asked, plane), 1.0, 0.0
    ).astype(BF16)
    return split_dot(chosen, values, ((0,), (0,)))


def pick_kernel(planes, place, asked, *refs):
    out = refs[-1]
    plane = lax.div(place[0], PLANE)
    for n, away in enumerate(planes):
        got = pick_from(asked, (plane + away + RING) & (RING - 1), refs[n][...])
        for d in range(PLANE):
            out[d, n * USED : (n + 1) * USED, :] = got[d * SLOTS : d * SLOTS + USED]


def held_kernel(*refs):
    pass


def hold(arrays, *until, wait=0):
    n = len(arrays)
    return pl.pallas_call(
        held_kernel,
        out_shape=tuple(shape(*a.shape) for a in arrays),
        in_specs=[pl.BlockSpec(memory_space=pl.ANY)] * (n + len(until)),
        out_specs=(pl.BlockSpec(memory_space=pl.ANY),) * n,
        input_output_aliases={i: i for i in range(n)},
        cost_estimate=pl.CostEstimate(flops=wait * 10**9, bytes_accessed=0, transcendentals=0),
    )(*arrays, *until)


def token_kernel(*refs):
    refs[-1][...] = jnp.zeros((8, 128), F32)


def token(arrays, wait):
    return call(
        token_kernel,
        shape(8, 128),
        in_specs=[pl.BlockSpec(memory_space=pl.ANY)] * len(arrays),
        flops=wait * 10**9,
    )(*arrays)


def far_dot(at, far):
    rows = far.shape[0] * far.shape[1]
    chosen = jnp.where(
        lax.broadcasted_iota(I32, (FINE, rows), 1) == at, 1.0 - own_share, 0.0
    ).astype(BF16)
    return split_dot(chosen, far.reshape(rows, far.shape[2]))


def far_part(codes, lane, far, low, high):
    at = codes[:, lane : lane + 1]
    xy, row = at >> 7, at & 127
    here = (at >= 0) & (row >= low) & (row < high)
    at = jnp.where(here, xy * (high - low) + row - low, -1)
    return far_dot(at, far[:, low:high, :])


def near_part(near):
    own = lax.broadcasted_iota(I32, (FINE, ROWS), 0) >> 1
    chosen = jnp.where(
        lax.broadcasted_iota(I32, (FINE, ROWS), 1) == own, own_share, 0.0
    ).astype(BF16)
    return split_dot(chosen, near[...])


def gather_kernel(parts, codes, near, *refs):
    total = near_part(near)
    for lane, exchange, low, high in parts:
        total = total + far_part(codes, lane, refs[exchange], low, high)
    refs[-1][...] = total


def final_kernel(codes, *refs):
    first_half = pl.program_id(0) < 2
    at = jnp.where(first_half, codes[:, 3:4], codes[:, 7:8])
    at = jnp.where(at >= 0, (at >> 7) * SENT + (at & 127), -1)
    rows = PLANE * SENT
    chosen = jnp.where(
        lax.broadcasted_iota(I32, (FINE, rows), 1) == at, 1.0 - own_share, 0.0
    ).astype(BF16)
    row = lax.broadcasted_iota(I32, (256, 256), 0) & 127
    lane = lax.broadcasted_iota(I32, (256, 256), 1) >> 1
    twice = jnp.where(row == lane, 1.0, 0.0).astype(BF16)
    far = [piece for k in range(3) for piece in halves(refs[6 + k][...].reshape(rows, 128))]
    far = jnp.dot(chosen, jnp.concatenate(far, axis=1), preferred_element_type=F32)
    for state in range(3):
        acc0, acc1, out = (refs[3 * k + state] for k in (0, 1, 3))
        at = state * 256
        mixed = jnp.where(first_half, acc0[...], acc1[...])
        mixed = mixed + far[:, at : at + 128] + far[:, at + 128 : at + 256]
        out[...] = jnp.dot(
            jnp.concatenate(halves(mixed), axis=1), twice, preferred_element_type=F32
        )


PLANES = [[z * PLANE + p for p in range(PLANE)] for z in range(RING)]
UP = [(z * PLANE + p, ((z + 1) % RING) * PLANE + p) for z in range(RING) for p in range(PLANE)]
DOWN = [(b, a) for a, b in UP]
CORE = [(0, 1), (1, 0), (2, 3), (3, 2)]
NEXT_Y = [(0, 2), (2, 0), (1, 3), (3, 1)]


def on_device(grad_parts, weight, first, second, partner_device, partner_column):
    place = jnp.stack([lax.axis_index("shard"), lax.axis_index("dp")]).astype(I32)
    grad = grad_parts[0]

    wanted, codes = call(
        index_kernel,
        (shape(PLANE, RING, 128, dtype=I32), shape(FINE, 128, dtype=I32)),
        in_specs=[scalar(), whole(), whole(), whole()],
        moved=1 << 20,
    )(
        place,
        partner_device,
        partner_device.reshape(1, FINE),
        partner_column.reshape(FINE, 1),
    )
    asked = lax.all_to_all(
        wanted, "shard", split_axis=0, concat_axis=0, axis_index_groups=PLANES, tiled=True
    )
    sends = call(
        send_core_kernel,
        (shape(ROWS, 2 * HALF),) * 2,
        in_specs=[scalar(), whole()],
        moved=3 << 20,
    )(place, grad)
    got_core = [lax.ppermute(s, "dp", CORE) for s in sends]
    state = []
    for half in range(2):
        got = got_core[half]
        passed = call(
            lambda *refs, half=half: send_y_kernel(half, *refs),
            shape(ROWS, HALF),
            grid=(1,),
            in_specs=[
                scalar(),
                pl.BlockSpec((ROWS, 4 * FEATS), lambda i: (0, 0)),
                pl.BlockSpec((ROWS, HALF), lambda i: (0, 0)),
            ],
            out_specs=pl.BlockSpec((ROWS, HALF), lambda i: (0, 0)),
            moved=1 << 20,
        )(place, grad, got)
        got_y = lax.ppermute(passed, "dp", NEXT_Y)
        block = pl.BlockSpec((ROWS, HALF), lambda i, half=half: (0, half))
        state.append(
            call(
                lambda *refs, half=half: update_kernel(half, *refs),
                shape(ROWS, WIDE),
                grid=(1,),
                in_specs=[
                    scalar(),
                    pl.BlockSpec((ROWS, 4 * FEATS), lambda i: (0, 0)),
                    pl.BlockSpec((ROWS, HALF), lambda i: (0, 1)),
                    pl.BlockSpec((ROWS, HALF), lambda i: (0, 0)),
                    block,
                    block,
                    block,
                ]
                + [pl.BlockSpec(memory_space=pl.ANY)] * half,
                out_specs=pl.BlockSpec((ROWS, WIDE), lambda i: (0, 0)),
                moved=2 << 20,
            )(place, grad, got, got_y, weight, first, second, *[wanted] * half)
        )

    def pick(planes, sources, wait, after=()):
        if wait:
            after = (*after, token(sources, wait))
        return call(
            lambda *refs: pick_kernel(planes, *refs),
            shape(PLANE, SENT, WIDE),
            in_specs=[scalar()]
            + [whole()] * (1 + len(sources))
            + [pl.BlockSpec(memory_space=pl.ANY)] * len(after),
            flops=4 * SLOTS * PLANE * ROWS * WIDE * 4,
            moved=5 << 20,
        )(place, asked, *sources, *after)

    def to_plane(rows):
        return lax.all_to_all(
            rows, "shard", split_axis=0, concat_axis=0, axis_index_groups=PLANES, tiled=True
        )

    def around(pair):
        return lax.ppermute(pair[0], "shard", UP), lax.ppermute(pair[1], "shard", DOWN)

    one = [around((x, x)) for x in state]
    rows = pick((0, 0, -1, 1), (*state, *one[0]), 10)
    far1 = to_plane(rows)
    one = [hold(one[0], rows), hold(one[1], wait=10)]
    two = [around(pair) for pair in one]
    three = [around(pair) for pair in two]
    four = (
        lax.ppermute(three[0][0], "shard", UP),
        lax.ppermute(three[1][1], "shard", DOWN),
    )
    far2 = to_plane(pick((-1, 1, -2, 2), (*one[1], *two[0]), 5, (far1,)))
    far3 = to_plane(pick((-2, 2, -3, 3), (*two[1], *three[0]), 10, (far2,)))
    far4 = to_plane(pick((-3, 3, 4, 4), (*three[1], *four), 10, (far3,)))

    acc = []
    for half, parts in enumerate(
        (
            ((0, 0, 0, 56), (1, 1, 24, 56), (2, 2, 24, 56)),
            ((4, 0, 8, 32), (5, 1, 0, 32), (6, 2, 0, 32)),
        )
    ):
        acc.append(
            call(
                lambda *refs, parts=parts: gather_kernel(parts, *refs),
                shape(FINE, WIDE),
                grid=(3,),
                in_specs=[
                    pl.BlockSpec((FINE, 128), lambda i: (0, 0)),
                    pl.BlockSpec((ROWS, HALF), lambda i: (0, i)),
                ]
                + [pl.BlockSpec((PLANE, SENT, HALF), lambda i: (0, 0, i))] * 3,
                out_specs=pl.BlockSpec((FINE, HALF), lambda i: (0, i)),
                flops=FINE * 1120 * WIDE * 4,
                moved=8 << 20,
            )(codes, state[half], far1, far2, far3)
        )

    def acc_block(half, state):
        def index(j):
            k = jnp.minimum(j, 1) if half == 0 else jnp.maximum(j - 2, 0)
            return 0, state * 2 + k

        return pl.BlockSpec((FINE, 128), index)

    def far_block(state):
        return pl.BlockSpec((PLANE, SENT, 128), lambda j: (0, 0, state * 2 + lax.rem(j, 2)))

    return call(
        final_kernel,
        (shape(FINE, 2 * FEATS),) * 3,
        grid=(4,),
        in_specs=[pl.BlockSpec((FINE, 128), lambda j: (0, 0))]
        + [acc_block(half, s) for half in range(2) for s in range(3)]
        + [far_block(s) for s in range(3)],
        out_specs=(pl.BlockSpec((FINE, 256), lambda j: (0, j)),) * 3,
        flops=FINE * 512 * 1536 * 4,
        moved=12 << 20,
    )(codes, acc[0], acc[0], acc[0], acc[1], acc[1], acc[1], far4, far4, far4)


def solution(mesh):
    placed = (
        P("dp", "shard", None),
        P("shard", "dp"),
        P("shard", "dp"),
        P("shard", "dp"),
        P("shard", None),
        P("shard"),
    )
    return jax.shard_map(
        on_device,
        mesh=mesh,
        in_specs=placed,
        out_specs=(P("shard", "dp"), P("shard", "dp"), P("shard", "dp")),
        check_vma=False,
    )
```

```python
import jax
import jax.numpy as jnp
from jax import lax
from jax.experimental import pallas as pl
from jax.experimental.pallas import tpu as pltpu
from jax.sharding import PartitionSpec as P

STEP = 20

first_decay = 0.9
second_decay = 0.95
learning_rate = 0.02
weight_decay = 0.1
epsilon = 1e-08
own_share = 0.75

F32 = jnp.float32
BF16 = jnp.bfloat16
I32 = jnp.int32

ROWS = 224
FINE = 448
FEATS = 512
HALF = 256
WIDE = 3 * HALF
SLOTS = 16
USED = 14
SENT = 4 * USED
PLANE = 8
RING = 8

VMEM = pltpu.CompilerParams(vmem_limit_bytes=12 * 1024 * 1024)


def call(kernel, out, *, grid=None, in_specs=None, out_specs=None, flops=0, moved=0, aliases=None):
    extra = {}
    if grid is not None:
        extra = dict(grid=grid, in_specs=in_specs, out_specs=out_specs)
    elif in_specs is not None:
        extra = dict(in_specs=in_specs)
    return pl.pallas_call(
        kernel,
        out_shape=out,
        compiler_params=VMEM,
        input_output_aliases=aliases or {},
        cost_estimate=pl.CostEstimate(flops=flops, bytes_accessed=moved, transcendentals=0),
        **extra,
    )


def shape(*dims, dtype=F32):
    return jax.ShapeDtypeStruct(dims, dtype)


def whole():
    return pl.BlockSpec(memory_space=pltpu.VMEM)


def scalar():
    return pl.BlockSpec(memory_space=pltpu.SMEM)


def halves(values):
    high = values.astype(BF16)
    return high, (values - high.astype(F32)).astype(BF16)


def split_dot(chosen, values, contract=((1,), (0,))):
    dims = (contract, ((), ()))
    high, low = halves(values)
    return lax.dot_general(chosen, high, dims, preferred_element_type=F32) + lax.dot_general(
        chosen, low, dims, preferred_element_type=F32
    )


def send_core_kernel(place, grad, out0, out1):
    dp = place[1]
    core, y = lax.rem(dp, 2), lax.div(dp, 2)
    for half, out in enumerate((out0, out1)):
        for part, row in enumerate((1 - y, y)):
            at = pl.multiple_of((row * 2 + 1 - core) * FEATS + half * HALF, HALF)
            out[:, part * HALF : (part + 1) * HALF] = grad[:, pl.ds(at, HALF)].astype(F32)


def send_y_kernel(half, place, grad, got, out):
    dp = place[1]
    core, y = lax.rem(dp, 2), lax.div(dp, 2)
    at = pl.multiple_of(((1 - y) * 2 + core) * FEATS + half * HALF, HALF)
    out[...] = grad[:, pl.ds(at, HALF)].astype(F32) + got[...]


def update_kernel(half, place, grad, got, got_y, weight, first, second, *refs):
    out = refs[-1]
    dp = place[1]
    at = pl.multiple_of(dp * FEATS + half * HALF, HALF)
    total = grad[:, pl.ds(at, HALF)].astype(F32) + got[...] + got_y[...]
    new_first = first_decay * first[...] + (1.0 - first_decay) * total
    new_second = second_decay * second[...] + (1.0 - second_decay) * total * total
    first_hat = new_first / (1.0 - first_decay**STEP)
    second_hat = new_second / (1.0 - second_decay**STEP)
    old = weight[...]
    new_weight = old - learning_rate * (
        first_hat / (jnp.sqrt(second_hat) + epsilon) + weight_decay * old
    )
    out[:, 0:HALF] = new_weight
    out[:, HALF : 2 * HALF] = new_first
    out[:, 2 * HALF : 3 * HALF] = new_second


def index_kernel(place, dev, dev_row, col, wanted, codes):
    shard = place[0]
    plane, me = lax.div(shard, PLANE), lax.rem(shard, PLANE)
    d = dev[...]
    r = dev_row[...]
    earlier = lax.broadcasted_iota(I32, (FINE, FINE), 1) < lax.broadcasted_iota(
        I32, (FINE, FINE), 0
    )
    slot = jnp.sum(jnp.where(earlier & (d == r), 1, 0), axis=1, keepdims=True)
    source_xy, source_z = d & (PLANE - 1), d >> 3
    row_of = ((r & (PLANE - 1)) << 3) + (r >> 3)
    left = jnp.where(lax.broadcasted_iota(I32, (64, FINE), 0) == row_of, 1.0, 0.0).astype(BF16)
    right = jnp.where(
        lax.broadcasted_iota(I32, (FINE, 128), 1) == me * SLOTS + slot, col[...].astype(F32), 0.0
    ).astype(BF16)
    table = jnp.dot(left, right, preferred_element_type=F32)
    wanted[...] = table.astype(I32).reshape(PLANE, RING, 128)
    away = (source_z - plane + RING) & (RING - 1)
    none = -1

    def place_in(offsets):
        at = jnp.full((FINE, 1), none, I32)
        for k, offset in offsets:
            at = jnp.where(away == k, source_xy * 128 + offset + slot, at)
        return at

    groups = (
        place_in(((0, 0), (7, 28), (1, 42))),
        place_in(((6, 28), (2, 42))),
        place_in(((5, 28), (3, 42))),
        place_in(((4, 28),)),
        place_in(((0, 14),)),
        place_in(((7, 0), (1, 14))),
        place_in(((6, 0), (2, 14))),
        place_in(((5, 0), (3, 14), (4, 42))),
    )
    lane = lax.broadcasted_iota(I32, (FINE, 128), 1)
    out = jnp.full((FINE, 128), none, I32)
    for g, at in enumerate(groups):
        out = jnp.where(lane == g, at, out)
    codes[...] = out


def asked_rows(asked, plane):
    here = lax.broadcasted_iota(I32, (RING, 128), 0) == plane
    return jnp.sum(jnp.where(here, jnp.sum(asked[...], axis=0), 0), axis=0, keepdims=True)


def pick_from(asked, plane, values):
    rows = values.shape[0]
    chosen = jnp.where(
        lax.broadcasted_iota(I32, (rows, 128), 0) == asked_rows(asked, plane), 1.0, 0.0
    ).astype(BF16)
    return split_dot(chosen, values, ((0,), (0,)))


def pick_kernel(planes, place, asked, *refs):
    out = refs[-1]
    plane = lax.div(place[0], PLANE)
    for n, away in enumerate(planes):
        got = pick_from(asked, (plane + away + RING) & (RING - 1), refs[n][...])
        for d in range(PLANE):
            out[d, n * USED : (n + 1) * USED, :] = got[d * SLOTS : d * SLOTS + USED]


def held_kernel(*refs):
    pass


def hold(arrays, *until, wait=0):
    n = len(arrays)
    return pl.pallas_call(
        held_kernel,
        out_shape=tuple(shape(*a.shape) for a in arrays),
        in_specs=[pl.BlockSpec(memory_space=pl.ANY)] * (n + len(until)),
        out_specs=(pl.BlockSpec(memory_space=pl.ANY),) * n,
        input_output_aliases={i: i for i in range(n)},
        cost_estimate=pl.CostEstimate(flops=wait * 10**9, bytes_accessed=0, transcendentals=0),
    )(*arrays, *until)


def token_kernel(*refs):
    refs[-1][...] = jnp.zeros((8, 128), F32)


def token(arrays, wait):
    return call(
        token_kernel,
        shape(8, 128),
        in_specs=[pl.BlockSpec(memory_space=pl.ANY)] * len(arrays),
        flops=wait * 10**9,
    )(*arrays)


def far_dot(at, far):
    rows = far.shape[0] * far.shape[1]
    chosen = jnp.where(
        lax.broadcasted_iota(I32, (FINE, rows), 1) == at, 1.0 - own_share, 0.0
    ).astype(BF16)
    return split_dot(chosen, far.reshape(rows, far.shape[2]))


def far_part(codes, lane, far, low, high):
    at = codes[:, lane : lane + 1]
    xy, row = at >> 7, at & 127
    here = (at >= 0) & (row >= low) & (row < high)
    at = jnp.where(here, xy * (high - low) + row - low, -1)
    return far_dot(at, far[:, low:high, :])


def near_part(near):
    own = lax.broadcasted_iota(I32, (FINE, ROWS), 0) >> 1
    chosen = jnp.where(
        lax.broadcasted_iota(I32, (FINE, ROWS), 1) == own, own_share, 0.0
    ).astype(BF16)
    return split_dot(chosen, near[...])


def gather_kernel(parts, codes, near, *refs):
    total = near_part(near)
    for lane, exchange, low, high in parts:
        total = total + far_part(codes, lane, refs[exchange], low, high)
    refs[-1][...] = total


def final_kernel(codes, *refs):
    first_half = pl.program_id(0) < 2
    at = jnp.where(first_half, codes[:, 3:4], codes[:, 7:8])
    at = jnp.where(at >= 0, (at >> 7) * SENT + (at & 127), -1)
    rows = PLANE * SENT
    chosen = jnp.where(
        lax.broadcasted_iota(I32, (FINE, rows), 1) == at, 1.0 - own_share, 0.0
    ).astype(BF16)
    row = lax.broadcasted_iota(I32, (256, 256), 0) & 127
    lane = lax.broadcasted_iota(I32, (256, 256), 1) >> 1
    twice = jnp.where(row == lane, 1.0, 0.0).astype(BF16)
    far = [piece for k in range(3) for piece in halves(refs[6 + k][...].reshape(rows, 128))]
    far = jnp.dot(chosen, jnp.concatenate(far, axis=1), preferred_element_type=F32)
    for state in range(3):
        acc0, acc1, out = (refs[3 * k + state] for k in (0, 1, 3))
        at = state * 256
        mixed = jnp.where(first_half, acc0[...], acc1[...])
        mixed = mixed + far[:, at : at + 128] + far[:, at + 128 : at + 256]
        out[...] = jnp.dot(
            jnp.concatenate(halves(mixed), axis=1), twice, preferred_element_type=F32
        )


PLANES = [[z * PLANE + p for p in range(PLANE)] for z in range(RING)]
UP = [(z * PLANE + p, ((z + 1) % RING) * PLANE + p) for z in range(RING) for p in range(PLANE)]
DOWN = [(b, a) for a, b in UP]
CORE = [(0, 1), (1, 0), (2, 3), (3, 2)]
NEXT_Y = [(0, 2), (2, 0), (1, 3), (3, 1)]


def on_device(grad_parts, weight, first, second, partner_device, partner_column):
    place = jnp.stack([lax.axis_index("shard"), lax.axis_index("dp")]).astype(I32)
    grad = grad_parts[0]

    wanted, codes = call(
        index_kernel,
        (shape(PLANE, RING, 128, dtype=I32), shape(FINE, 128, dtype=I32)),
        in_specs=[scalar(), whole(), whole(), whole()],
        moved=1 << 20,
    )(
        place,
        partner_device,
        partner_device.reshape(1, FINE),
        partner_column.reshape(FINE, 1),
    )
    asked = lax.all_to_all(
        wanted, "shard", split_axis=0, concat_axis=0, axis_index_groups=PLANES, tiled=True
    )
    sends = call(
        send_core_kernel,
        (shape(ROWS, 2 * HALF),) * 2,
        in_specs=[scalar(), whole()],
        moved=3 << 20,
    )(place, grad)
    got_core = [lax.ppermute(s, "dp", CORE) for s in sends]
    state = []
    for half in range(2):
        got = got_core[half]
        passed = call(
            lambda *refs, half=half: send_y_kernel(half, *refs),
            shape(ROWS, HALF),
            grid=(1,),
            in_specs=[
                scalar(),
                pl.BlockSpec((ROWS, 4 * FEATS), lambda i: (0, 0)),
                pl.BlockSpec((ROWS, HALF), lambda i: (0, 0)),
            ],
            out_specs=pl.BlockSpec((ROWS, HALF), lambda i: (0, 0)),
            moved=1 << 20,
        )(place, grad, got)
        got_y = lax.ppermute(passed, "dp", NEXT_Y)
        block = pl.BlockSpec((ROWS, HALF), lambda i, half=half: (0, half))
        state.append(
            call(
                lambda *refs, half=half: update_kernel(half, *refs),
                shape(ROWS, WIDE),
                grid=(1,),
                in_specs=[
                    scalar(),
                    pl.BlockSpec((ROWS, 4 * FEATS), lambda i: (0, 0)),
                    pl.BlockSpec((ROWS, HALF), lambda i: (0, 1)),
                    pl.BlockSpec((ROWS, HALF), lambda i: (0, 0)),
                    block,
                    block,
                    block,
                ]
                + [pl.BlockSpec(memory_space=pl.ANY)] * half,
                out_specs=pl.BlockSpec((ROWS, WIDE), lambda i: (0, 0)),
                moved=2 << 20,
            )(place, grad, got, got_y, weight, first, second, *[wanted] * half)
        )

    def pick(planes, sources, wait, after=()):
        if wait:
            after = (*after, token(sources, wait))
        return call(
            lambda *refs: pick_kernel(planes, *refs),
            shape(PLANE, SENT, WIDE),
            in_specs=[scalar()]
            + [whole()] * (1 + len(sources))
            + [pl.BlockSpec(memory_space=pl.ANY)] * len(after),
            flops=4 * SLOTS * PLANE * ROWS * WIDE * 4,
            moved=5 << 20,
        )(place, asked, *sources, *after)

    def to_plane(rows):
        return lax.all_to_all(
            rows, "shard", split_axis=0, concat_axis=0, axis_index_groups=PLANES, tiled=True
        )

    def around(pair):
        return lax.ppermute(pair[0], "shard", UP), lax.ppermute(pair[1], "shard", DOWN)

    one = [around((x, x)) for x in state]
    rows = pick((0, 0, -1, 1), (*state, *one[0]), 4)
    far1 = to_plane(rows)
    one = [hold(one[0], rows), hold(one[1], wait=10)]
    two = [around(pair) for pair in one]
    rows = pick((-1, 1, -2, 2), (*one[1], *two[0]), 5, (far1,))
    far2 = to_plane(rows)
    two = [hold(two[0], rows), hold(two[1], wait=10)]
    three = [around(pair) for pair in two]
    rows = pick((-2, 2, -3, 3), (*two[1], *three[0]), 5, (far2,))
    far3 = to_plane(rows)
    three = [hold(three[0], rows), hold(three[1], wait=10)]
    four = (
        lax.ppermute(three[0][0], "shard", UP),
        lax.ppermute(three[1][1], "shard", DOWN),
    )
    far4 = to_plane(pick((-3, 3, 4, 4), (*three[1], *four), 5, (far3,)))

    acc = []
    for half, parts in enumerate(
        (
            ((0, 0, 0, 56), (1, 1, 24, 56), (2, 2, 24, 56)),
            ((4, 0, 8, 32), (5, 1, 0, 32), (6, 2, 0, 32)),
        )
    ):
        acc.append(
            call(
                lambda *refs, parts=parts: gather_kernel(parts, *refs),
                shape(FINE, WIDE),
                grid=(3,),
                in_specs=[
                    pl.BlockSpec((FINE, 128), lambda i: (0, 0)),
                    pl.BlockSpec((ROWS, HALF), lambda i: (0, i)),
                ]
                + [pl.BlockSpec((PLANE, SENT, HALF), lambda i: (0, 0, i))] * 3,
                out_specs=pl.BlockSpec((FINE, HALF), lambda i: (0, i)),
                flops=FINE * 1120 * WIDE * 4,
                moved=8 << 20,
            )(codes, state[half], far1, far2, far3)
        )

    def acc_block(half, state):
        def index(j):
            k = jnp.minimum(j, 1) if half == 0 else jnp.maximum(j - 2, 0)
            return 0, state * 2 + k

        return pl.BlockSpec((FINE, 128), index)

    def far_block(state):
        return pl.BlockSpec((PLANE, SENT, 128), lambda j: (0, 0, state * 2 + lax.rem(j, 2)))

    return call(
        final_kernel,
        (shape(FINE, 2 * FEATS),) * 3,
        grid=(4,),
        in_specs=[pl.BlockSpec((FINE, 128), lambda j: (0, 0))]
        + [acc_block(half, s) for half in range(2) for s in range(3)]
        + [far_block(s) for s in range(3)],
        out_specs=(pl.BlockSpec((FINE, 256), lambda j: (0, j)),) * 3,
        flops=FINE * 512 * 1536 * 4,
        moved=12 << 20,
    )(codes, acc[0], acc[0], acc[0], acc[1], acc[1], acc[1], far4, far4, far4)


def solution(mesh):
    placed = (
        P("dp", "shard", None),
        P("shard", "dp"),
        P("shard", "dp"),
        P("shard", "dp"),
        P("shard", None),
        P("shard"),
    )
    return jax.shard_map(
        on_device,
        mesh=mesh,
        in_specs=placed,
        out_specs=(P("shard", "dp"), P("shard", "dp"), P("shard", "dp")),
        check_vma=False,
    )
```

```python
import jax
import jax.numpy as jnp
from jax import lax
from jax.experimental import pallas as pl
from jax.experimental.pallas import tpu as pltpu
from jax.sharding import PartitionSpec as P

STEP = 20

first_decay = 0.9
second_decay = 0.95
learning_rate = 0.02
weight_decay = 0.1
epsilon = 1e-08
own_share = 0.75

F32 = jnp.float32
BF16 = jnp.bfloat16
I32 = jnp.int32

ROWS = 224
FINE = 448
FEATS = 512
HALF = 256
WIDE = 3 * HALF
SLOTS = 16
USED = 14
SENT = 4 * USED
PLANE = 8
RING = 8

VMEM = pltpu.CompilerParams(vmem_limit_bytes=12 * 1024 * 1024)


def call(kernel, out, *, grid=None, in_specs=None, out_specs=None, flops=0, moved=0, aliases=None):
    extra = {}
    if grid is not None:
        extra = dict(grid=grid, in_specs=in_specs, out_specs=out_specs)
    elif in_specs is not None:
        extra = dict(in_specs=in_specs)
    return pl.pallas_call(
        kernel,
        out_shape=out,
        compiler_params=VMEM,
        input_output_aliases=aliases or {},
        cost_estimate=pl.CostEstimate(flops=flops, bytes_accessed=moved, transcendentals=0),
        **extra,
    )


def shape(*dims, dtype=F32):
    return jax.ShapeDtypeStruct(dims, dtype)


def whole():
    return pl.BlockSpec(memory_space=pltpu.VMEM)


def scalar():
    return pl.BlockSpec(memory_space=pltpu.SMEM)


def halves(values):
    high = values.astype(BF16)
    return high, (values - high.astype(F32)).astype(BF16)


def split_dot(chosen, values, contract=((1,), (0,))):
    dims = (contract, ((), ()))
    high, low = halves(values)
    return lax.dot_general(chosen, high, dims, preferred_element_type=F32) + lax.dot_general(
        chosen, low, dims, preferred_element_type=F32
    )


def send_core_kernel(place, grad, out0, out1):
    dp = place[1]
    core, y = lax.rem(dp, 2), lax.div(dp, 2)
    for half, out in enumerate((out0, out1)):
        for part, row in enumerate((1 - y, y)):
            at = pl.multiple_of((row * 2 + 1 - core) * FEATS + half * HALF, HALF)
            out[:, part * HALF : (part + 1) * HALF] = grad[:, pl.ds(at, HALF)].astype(F32)


def send_y_kernel(half, place, grad, got, out):
    dp = place[1]
    core, y = lax.rem(dp, 2), lax.div(dp, 2)
    at = pl.multiple_of(((1 - y) * 2 + core) * FEATS + half * HALF, HALF)
    out[...] = grad[:, pl.ds(at, HALF)].astype(F32) + got[...]


def update_kernel(half, place, grad, got, got_y, weight, first, second, *refs):
    out = refs[-1]
    dp = place[1]
    at = pl.multiple_of(dp * FEATS + half * HALF, HALF)
    total = grad[:, pl.ds(at, HALF)].astype(F32) + got[...] + got_y[...]
    new_first = first_decay * first[...] + (1.0 - first_decay) * total
    new_second = second_decay * second[...] + (1.0 - second_decay) * total * total
    first_hat = new_first / (1.0 - first_decay**STEP)
    second_hat = new_second / (1.0 - second_decay**STEP)
    old = weight[...]
    new_weight = old - learning_rate * (
        first_hat / (jnp.sqrt(second_hat) + epsilon) + weight_decay * old
    )
    out[:, 0:HALF] = new_weight
    out[:, HALF : 2 * HALF] = new_first
    out[:, 2 * HALF : 3 * HALF] = new_second


def index_kernel(place, dev, dev_row, col, wanted, codes):
    shard = place[0]
    plane, me = lax.div(shard, PLANE), lax.rem(shard, PLANE)
    d = dev[...]
    r = dev_row[...]
    earlier = lax.broadcasted_iota(I32, (FINE, FINE), 1) < lax.broadcasted_iota(
        I32, (FINE, FINE), 0
    )
    slot = jnp.sum(jnp.where(earlier & (d == r), 1, 0), axis=1, keepdims=True)
    source_xy, source_z = d & (PLANE - 1), d >> 3
    row_of = ((r & (PLANE - 1)) << 3) + (r >> 3)
    left = jnp.where(lax.broadcasted_iota(I32, (64, FINE), 0) == row_of, 1.0, 0.0).astype(BF16)
    right = jnp.where(
        lax.broadcasted_iota(I32, (FINE, 128), 1) == me * SLOTS + slot, col[...].astype(F32), 0.0
    ).astype(BF16)
    table = jnp.dot(left, right, preferred_element_type=F32)
    wanted[...] = table.astype(I32).reshape(PLANE, RING, 128)
    away = (source_z - plane + RING) & (RING - 1)
    none = -1

    def place_in(offsets):
        at = jnp.full((FINE, 1), none, I32)
        for k, offset in offsets:
            at = jnp.where(away == k, source_xy * 128 + offset + slot, at)
        return at

    groups = (
        place_in(((0, 0), (7, 28), (1, 42))),
        place_in(((6, 28), (2, 42))),
        place_in(((5, 28), (3, 42))),
        place_in(((4, 28),)),
        place_in(((0, 14),)),
        place_in(((7, 0), (1, 14))),
        place_in(((6, 0), (2, 14))),
        place_in(((5, 0), (3, 14), (4, 42))),
    )
    lane = lax.broadcasted_iota(I32, (FINE, 128), 1)
    out = jnp.full((FINE, 128), none, I32)
    for g, at in enumerate(groups):
        out = jnp.where(lane == g, at, out)
    codes[...] = out


def asked_rows(asked, plane):
    here = lax.broadcasted_iota(I32, (RING, 128), 0) == plane
    return jnp.sum(jnp.where(here, jnp.sum(asked[...], axis=0), 0), axis=0, keepdims=True)


def pick_from(asked, plane, values):
    rows = values.shape[0]
    chosen = jnp.where(
        lax.broadcasted_iota(I32, (rows, 128), 0) == asked_rows(asked, plane), 1.0, 0.0
    ).astype(BF16)
    return split_dot(chosen, values, ((0,), (0,)))


def pick_kernel(planes, place, asked, *refs):
    out = refs[-1]
    plane = lax.div(place[0], PLANE)
    for n, away in enumerate(planes):
        got = pick_from(asked, (plane + away + RING) & (RING - 1), refs[n][...])
        for d in range(PLANE):
            out[d, n * USED : (n + 1) * USED, :] = got[d * SLOTS : d * SLOTS + USED]


def held_kernel(*refs):
    pass


def hold(arrays, *until, wait=0):
    n = len(arrays)
    return pl.pallas_call(
        held_kernel,
        out_shape=tuple(shape(*a.shape) for a in arrays),
        in_specs=[pl.BlockSpec(memory_space=pl.ANY)] * (n + len(until)),
        out_specs=(pl.BlockSpec(memory_space=pl.ANY),) * n,
        input_output_aliases={i: i for i in range(n)},
        cost_estimate=pl.CostEstimate(flops=wait * 10**9, bytes_accessed=0, transcendentals=0),
    )(*arrays, *until)


def token_kernel(*refs):
    refs[-1][...] = jnp.zeros((8, 128), F32)


def token(arrays, wait):
    return call(
        token_kernel,
        shape(8, 128),
        in_specs=[pl.BlockSpec(memory_space=pl.ANY)] * len(arrays),
        flops=wait * 10**9,
    )(*arrays)


def far_dot(at, far):
    rows = far.shape[0] * far.shape[1]
    chosen = jnp.where(
        lax.broadcasted_iota(I32, (FINE, rows), 1) == at, 1.0 - own_share, 0.0
    ).astype(BF16)
    return split_dot(chosen, far.reshape(rows, far.shape[2]))


def far_part(codes, lane, far, low, high):
    at = codes[:, lane : lane + 1]
    xy, row = at >> 7, at & 127
    here = (at >= 0) & (row >= low) & (row < high)
    at = jnp.where(here, xy * (high - low) + row - low, -1)
    return far_dot(at, far[:, low:high, :])


def near_part(near):
    own = lax.broadcasted_iota(I32, (FINE, ROWS), 0) >> 1
    chosen = jnp.where(
        lax.broadcasted_iota(I32, (FINE, ROWS), 1) == own, own_share, 0.0
    ).astype(BF16)
    return split_dot(chosen, near[...])


def gather_kernel(parts, codes, near, *refs):
    total = near_part(near)
    for lane, exchange, low, high in parts:
        total = total + far_part(codes, lane, refs[exchange], low, high)
    refs[-1][...] = total


def final_kernel(codes, *refs):
    first_half = pl.program_id(0) < 2
    at = jnp.where(first_half, codes[:, 3:4], codes[:, 7:8])
    at = jnp.where(at >= 0, (at >> 7) * SENT + (at & 127), -1)
    rows = PLANE * SENT
    chosen = jnp.where(
        lax.broadcasted_iota(I32, (FINE, rows), 1) == at, 1.0 - own_share, 0.0
    ).astype(BF16)
    row = lax.broadcasted_iota(I32, (256, 256), 0) & 127
    lane = lax.broadcasted_iota(I32, (256, 256), 1) >> 1
    twice = jnp.where(row == lane, 1.0, 0.0).astype(BF16)
    far = [piece for k in range(3) for piece in halves(refs[6 + k][...].reshape(rows, 128))]
    far = jnp.dot(chosen, jnp.concatenate(far, axis=1), preferred_element_type=F32)
    for state in range(3):
        acc0, acc1, out = (refs[3 * k + state] for k in (0, 1, 3))
        at = state * 256
        mixed = jnp.where(first_half, acc0[...], acc1[...])
        mixed = mixed + far[:, at : at + 128] + far[:, at + 128 : at + 256]
        out[...] = jnp.dot(
            jnp.concatenate(halves(mixed), axis=1), twice, preferred_element_type=F32
        )


PLANES = [[z * PLANE + p for p in range(PLANE)] for z in range(RING)]
UP = [(z * PLANE + p, ((z + 1) % RING) * PLANE + p) for z in range(RING) for p in range(PLANE)]
DOWN = [(b, a) for a, b in UP]
CORE = [(0, 1), (1, 0), (2, 3), (3, 2)]
NEXT_Y = [(0, 2), (2, 0), (1, 3), (3, 1)]


def on_device(grad_parts, weight, first, second, partner_device, partner_column):
    place = jnp.stack([lax.axis_index("shard"), lax.axis_index("dp")]).astype(I32)
    grad = grad_parts[0]

    wanted, codes = call(
        index_kernel,
        (shape(PLANE, RING, 128, dtype=I32), shape(FINE, 128, dtype=I32)),
        in_specs=[scalar(), whole(), whole(), whole()],
        moved=1 << 20,
    )(
        place,
        partner_device,
        partner_device.reshape(1, FINE),
        partner_column.reshape(FINE, 1),
    )
    asked = lax.all_to_all(
        wanted, "shard", split_axis=0, concat_axis=0, axis_index_groups=PLANES, tiled=True
    )
    sends = call(
        send_core_kernel,
        (shape(ROWS, 2 * HALF),) * 2,
        in_specs=[scalar(), whole()],
        moved=3 << 20,
    )(place, grad)
    got_core = [lax.ppermute(s, "dp", CORE) for s in sends]
    passed = [
        call(
            lambda *refs, half=half: send_y_kernel(half, *refs),
            shape(ROWS, HALF),
            grid=(1,),
            in_specs=[
                scalar(),
                pl.BlockSpec((ROWS, 4 * FEATS), lambda i: (0, 0)),
                pl.BlockSpec((ROWS, HALF), lambda i: (0, 0)),
            ],
            out_specs=pl.BlockSpec((ROWS, HALF), lambda i: (0, 0)),
            moved=1 << 20,
        )(place, grad, got_core[half])
        for half in range(2)
    ]
    got_y = [lax.ppermute(p, "dp", NEXT_Y) for p in passed]
    state = []
    for half in range(2):
        block = pl.BlockSpec((ROWS, HALF), lambda i, half=half: (0, half))
        after = (got_y[1], wanted) if half == 0 else ()
        state.append(
            call(
                lambda *refs, half=half: update_kernel(half, *refs),
                shape(ROWS, WIDE),
                grid=(1,),
                in_specs=[
                    scalar(),
                    pl.BlockSpec((ROWS, 4 * FEATS), lambda i: (0, 0)),
                    pl.BlockSpec((ROWS, HALF), lambda i: (0, 1)),
                    pl.BlockSpec((ROWS, HALF), lambda i: (0, 0)),
                    block,
                    block,
                    block,
                ]
                + [pl.BlockSpec(memory_space=pl.ANY)] * len(after),
                out_specs=pl.BlockSpec((ROWS, WIDE), lambda i: (0, 0)),
                moved=2 << 20,
            )(place, grad, got_core[half], got_y[half], weight, first, second, *after)
        )

    def pick(planes, sources, wait, after=()):
        if wait:
            after = (*after, token(sources, wait))
        return call(
            lambda *refs: pick_kernel(planes, *refs),
            shape(PLANE, SENT, WIDE),
            in_specs=[scalar()]
            + [whole()] * (1 + len(sources))
            + [pl.BlockSpec(memory_space=pl.ANY)] * len(after),
            flops=4 * SLOTS * PLANE * ROWS * WIDE * 4,
            moved=5 << 20,
        )(place, asked, *sources, *after)

    def to_plane(rows):
        return lax.all_to_all(
            rows, "shard", split_axis=0, concat_axis=0, axis_index_groups=PLANES, tiled=True
        )

    def around(pair):
        return lax.ppermute(pair[0], "shard", UP), lax.ppermute(pair[1], "shard", DOWN)

    one = [around((x, x)) for x in state]
    rows = pick((0, 0, -1, 1), (*state, *one[0]), 4)
    far1 = to_plane(rows)
    one = [hold(one[0], rows), hold(one[1], wait=10)]
    two = [around(pair) for pair in one]
    rows = pick((-1, 1, -2, 2), (*one[1], *two[0]), 5, (far1,))
    far2 = to_plane(rows)
    two = [hold(two[0], rows), hold(two[1], wait=10)]
    three = [around(pair) for pair in two]
    rows = pick((-2, 2, -3, 3), (*two[1], *three[0]), 5, (far2,))
    far3 = to_plane(rows)
    three = [hold(three[0], rows), hold(three[1], wait=10)]
    four = (
        lax.ppermute(three[0][0], "shard", UP),
        lax.ppermute(three[1][1], "shard", DOWN),
    )
    far4 = to_plane(pick((-3, 3, 4, 4), (*three[1], *four), 5, (far3,)))

    acc = []
    for half, parts in enumerate(
        (
            ((0, 0, 0, 56), (1, 1, 24, 56), (2, 2, 24, 56)),
            ((4, 0, 8, 32), (5, 1, 0, 32), (6, 2, 0, 32)),
        )
    ):
        acc.append(
            call(
                lambda *refs, parts=parts: gather_kernel(parts, *refs),
                shape(FINE, WIDE),
                grid=(3,),
                in_specs=[
                    pl.BlockSpec((FINE, 128), lambda i: (0, 0)),
                    pl.BlockSpec((ROWS, HALF), lambda i: (0, i)),
                ]
                + [pl.BlockSpec((PLANE, SENT, HALF), lambda i: (0, 0, i))] * 3,
                out_specs=pl.BlockSpec((FINE, HALF), lambda i: (0, i)),
                flops=FINE * 1120 * WIDE * 4,
                moved=8 << 20,
            )(codes, state[half], far1, far2, far3)
        )

    def acc_block(half, state):
        def index(j):
            k = jnp.minimum(j, 1) if half == 0 else jnp.maximum(j - 2, 0)
            return 0, state * 2 + k

        return pl.BlockSpec((FINE, 128), index)

    def far_block(state):
        return pl.BlockSpec((PLANE, SENT, 128), lambda j: (0, 0, state * 2 + lax.rem(j, 2)))

    return call(
        final_kernel,
        (shape(FINE, 2 * FEATS),) * 3,
        grid=(4,),
        in_specs=[pl.BlockSpec((FINE, 128), lambda j: (0, 0))]
        + [acc_block(half, s) for half in range(2) for s in range(3)]
        + [far_block(s) for s in range(3)],
        out_specs=(pl.BlockSpec((FINE, 256), lambda j: (0, j)),) * 3,
        flops=FINE * 512 * 1536 * 4,
        moved=12 << 20,
    )(codes, acc[0], acc[0], acc[0], acc[1], acc[1], acc[1], far4, far4, far4)


def solution(mesh):
    placed = (
        P("dp", "shard", None),
        P("shard", "dp"),
        P("shard", "dp"),
        P("shard", "dp"),
        P("shard", None),
        P("shard"),
    )
    return jax.shard_map(
        on_device,
        mesh=mesh,
        in_specs=placed,
        out_specs=(P("shard", "dp"), P("shard", "dp"), P("shard", "dp")),
        check_vma=False,
    )
```

```python
import jax
import jax.numpy as jnp
from jax import lax
from jax.experimental import pallas as pl
from jax.experimental.pallas import tpu as pltpu
from jax.sharding import PartitionSpec as P

STEP = 20

first_decay = 0.9
second_decay = 0.95
learning_rate = 0.02
weight_decay = 0.1
epsilon = 1e-08
own_share = 0.75

F32 = jnp.float32
BF16 = jnp.bfloat16
I32 = jnp.int32

ROWS = 224
FINE = 448
FEATS = 512
HALF = 256
WIDE = 3 * HALF
SLOTS = 16
USED = 14
SENT = 4 * USED
PLANE = 8
RING = 8

VMEM = pltpu.CompilerParams(vmem_limit_bytes=12 * 1024 * 1024)


def call(kernel, out, *, grid=None, in_specs=None, out_specs=None, flops=0, moved=0, aliases=None, scratch=()):
    extra = {}
    if grid is not None:
        extra = dict(grid=grid, in_specs=in_specs, out_specs=out_specs)
    elif in_specs is not None:
        extra = dict(in_specs=in_specs)
    return pl.pallas_call(
        kernel,
        out_shape=out,
        compiler_params=VMEM,
        input_output_aliases=aliases or {},
        scratch_shapes=scratch,
        cost_estimate=pl.CostEstimate(flops=flops, bytes_accessed=moved, transcendentals=0),
        **extra,
    )


def shape(*dims, dtype=F32):
    return jax.ShapeDtypeStruct(dims, dtype)


def whole():
    return pl.BlockSpec(memory_space=pltpu.VMEM)


def far_away():
    return pl.BlockSpec(memory_space=pltpu.HBM)


def scalar():
    return pl.BlockSpec(memory_space=pltpu.SMEM)


def halves(values):
    high = values.astype(BF16)
    return high, (values - high.astype(F32)).astype(BF16)


def split_dot(chosen, values, contract=((1,), (0,))):
    dims = (contract, ((), ()))
    high, low = halves(values)
    return lax.dot_general(chosen, high, dims, preferred_element_type=F32) + lax.dot_general(
        chosen, low, dims, preferred_element_type=F32
    )


def send_core_kernel(place, grad, out0, out1):
    dp = place[1]
    core, y = lax.rem(dp, 2), lax.div(dp, 2)
    for half, out in enumerate((out0, out1)):
        for part, row in enumerate((1 - y, y)):
            at = pl.multiple_of((row * 2 + 1 - core) * FEATS + half * HALF, HALF)
            out[:, part * HALF : (part + 1) * HALF] = grad[:, pl.ds(at, HALF)].astype(F32)


def send_y_kernel(half, place, grad, got, out):
    dp = place[1]
    core, y = lax.rem(dp, 2), lax.div(dp, 2)
    at = pl.multiple_of(((1 - y) * 2 + core) * FEATS + half * HALF, HALF)
    out[...] = grad[:, pl.ds(at, HALF)].astype(F32) + got[...]


def update_kernel(half, place, grad, got, got_y, weight, first, second, *refs):
    out, mine, held, done = refs[-4:]
    at = pl.multiple_of(place[1] * FEATS + half * HALF, HALF)
    here = pl.ds(half * HALF, HALF)
    copies = [pltpu.make_async_copy(grad.at[:, pl.ds(at, HALF)], mine, done.at[0])]
    for k, source in enumerate(
        (
            got.at[:, pl.ds(HALF, HALF)],
            got_y,
            first.at[:, here],
            second.at[:, here],
            weight.at[:, here],
        )
    ):
        copies.append(pltpu.make_async_copy(source, held.at[k], done.at[k + 1]))
    for copy in copies:
        copy.start()
    for copy in copies:
        copy.wait()
    got, got_y, first, second, weight = (held.at[k] for k in range(5))
    total = mine[...].astype(F32) + got[...] + got_y[...]
    new_first = first_decay * first[...] + (1.0 - first_decay) * total
    new_second = second_decay * second[...] + (1.0 - second_decay) * total * total
    first_hat = new_first / (1.0 - first_decay**STEP)
    second_hat = new_second / (1.0 - second_decay**STEP)
    old = weight[...]
    new_weight = old - learning_rate * (
        first_hat / (jnp.sqrt(second_hat) + epsilon) + weight_decay * old
    )
    out[:, 0:HALF] = new_weight
    out[:, HALF : 2 * HALF] = new_first
    out[:, 2 * HALF : 3 * HALF] = new_second


def index_kernel(place, dev, dev_row, col, wanted, codes):
    shard = place[0]
    plane, me = lax.div(shard, PLANE), lax.rem(shard, PLANE)
    d = dev[...]
    r = dev_row[...]
    earlier = lax.broadcasted_iota(I32, (FINE, FINE), 1) < lax.broadcasted_iota(
        I32, (FINE, FINE), 0
    )
    slot = jnp.sum(jnp.where(earlier & (d == r), 1, 0), axis=1, keepdims=True)
    later = lax.broadcasted_iota(I32, (FINE, FINE), 0) < lax.broadcasted_iota(
        I32, (FINE, FINE), 1
    )
    slot_row = jnp.sum(jnp.where(later & (d == r), 1, 0), axis=0, keepdims=True)
    source_xy, source_z = r & (PLANE - 1), r >> 3
    row_of = ((r & (PLANE - 1)) << 3) + (r >> 3)
    left = jnp.where(lax.broadcasted_iota(I32, (64, FINE), 0) == row_of, 1.0, 0.0).astype(BF16)
    right = jnp.where(
        lax.broadcasted_iota(I32, (FINE, 128), 1) == me * SLOTS + slot, col[...].astype(F32), 0.0
    ).astype(BF16)
    table = jnp.dot(left, right, preferred_element_type=F32)
    wanted[...] = table.astype(I32).reshape(PLANE, RING, 128)
    away = (source_z - plane + RING) & (RING - 1)
    none = -1

    def place_in(offsets):
        at = jnp.full((1, FINE), none, I32)
        for k, offset in offsets:
            at = jnp.where(away == k, source_xy * 128 + offset + slot_row, at)
        return at

    groups = (
        place_in(((0, 0), (7, 28), (1, 42))),
        place_in(((6, 28), (2, 42))),
        place_in(((5, 28), (3, 42))),
        place_in(((4, 28),)),
        place_in(((0, 14),)),
        place_in(((7, 0), (1, 14))),
        place_in(((6, 0), (2, 14))),
        place_in(((5, 0), (3, 14), (4, 42))),
    )
    codes[...] = jnp.concatenate(groups, axis=0)


def asked_rows(asked, plane):
    here = lax.broadcasted_iota(I32, (RING, 128), 0) == plane
    return jnp.sum(jnp.where(here, jnp.sum(asked[...], axis=0), 0), axis=0, keepdims=True)


def pick_from(asked, plane, values):
    rows = values.shape[0]
    chosen = jnp.where(
        lax.broadcasted_iota(I32, (rows, 128), 0) == asked_rows(asked, plane), 1.0, 0.0
    ).astype(BF16)
    return split_dot(chosen, values, ((0,), (0,)))


def pick_kernel(planes, place, asked, *refs):
    out, held, done = refs[-3:]
    plane = lax.div(place[0], PLANE)
    copies = [
        pltpu.make_async_copy(refs[n], held.at[n], done.at[n]) for n in range(len(planes))
    ]
    for copy in copies:
        copy.start()
    for n, away in enumerate(planes):
        copies[n].wait()
        got = pick_from(asked, (plane + away + RING) & (RING - 1), held[n])
        for d in range(PLANE):
            out[d, n * USED : (n + 1) * USED, :] = got[d * SLOTS : d * SLOTS + USED]


def held_kernel(*refs):
    pass


def hold(arrays, *until, wait=0):
    n = len(arrays)
    return pl.pallas_call(
        held_kernel,
        out_shape=tuple(shape(*a.shape) for a in arrays),
        in_specs=[pl.BlockSpec(memory_space=pl.ANY)] * (n + len(until)),
        out_specs=(pl.BlockSpec(memory_space=pl.ANY),) * n,
        input_output_aliases={i: i for i in range(n)},
        cost_estimate=pl.CostEstimate(flops=wait * 10**9, bytes_accessed=0, transcendentals=0),
    )(*arrays, *until)


def token_kernel(*refs):
    refs[-1][...] = jnp.zeros((8, 128), F32)


def token(arrays, wait):
    return call(
        token_kernel,
        shape(8, 128),
        in_specs=[pl.BlockSpec(memory_space=pl.ANY)] * len(arrays),
        flops=wait * 10**9,
    )(*arrays)


def far_dot(at, far):
    rows = far.shape[0] * far.shape[1]
    chosen = jnp.where(
        lax.broadcasted_iota(I32, (rows, FINE), 0) == at, 1.0 - own_share, 0.0
    ).astype(BF16)
    return split_dot(chosen, far.reshape(rows, far.shape[2]), ((0,), (0,)))


def far_part(codes, lane, far, low, high):
    at = codes[lane : lane + 1, :]
    xy, row = at >> 7, at & 127
    here = (at >= 0) & (row >= low) & (row < high)
    at = jnp.where(here, xy * (high - low) + row - low, -1)
    return far_dot(at, far[:, low:high, :])


def near_part(near):
    own = lax.broadcasted_iota(I32, (FINE, ROWS), 0) >> 1
    chosen = jnp.where(
        lax.broadcasted_iota(I32, (FINE, ROWS), 1) == own, own_share, 0.0
    ).astype(BF16)
    return split_dot(chosen, near[...])


def gather_kernel(parts, codes, near, *refs):
    total = near_part(near)
    for lane, exchange, low, high in parts:
        total = total + far_part(codes, lane, refs[exchange], low, high)
    refs[-1][...] = total


def final_kernel(codes, *refs):
    first_half = pl.program_id(0) < 2
    at = jnp.where(first_half, codes[3:4, :], codes[7:8, :])
    at = jnp.where(at >= 0, (at >> 7) * SENT + (at & 127), -1)
    rows = PLANE * SENT
    chosen = jnp.where(
        lax.broadcasted_iota(I32, (rows, FINE), 0) == at, 1.0 - own_share, 0.0
    ).astype(BF16)
    row = lax.broadcasted_iota(I32, (256, 256), 0) & 127
    lane = lax.broadcasted_iota(I32, (256, 256), 1) >> 1
    twice = jnp.where(row == lane, 1.0, 0.0).astype(BF16)
    far = [piece for k in range(3) for piece in halves(refs[6 + k][...].reshape(rows, 128))]
    far = lax.dot_general(
        chosen,
        jnp.concatenate(far, axis=1),
        (((0,), (0,)), ((), ())),
        preferred_element_type=F32,
    )
    for state in range(3):
        acc0, acc1, out = (refs[3 * k + state] for k in (0, 1, 3))
        at = state * 256
        mixed = jnp.where(first_half, acc0[...], acc1[...])
        mixed = mixed + far[:, at : at + 128] + far[:, at + 128 : at + 256]
        out[...] = jnp.dot(
            jnp.concatenate(halves(mixed), axis=1), twice, preferred_element_type=F32
        )


PLANES = [[z * PLANE + p for p in range(PLANE)] for z in range(RING)]
UP = [(z * PLANE + p, ((z + 1) % RING) * PLANE + p) for z in range(RING) for p in range(PLANE)]
DOWN = [(b, a) for a, b in UP]
CORE = [(0, 1), (1, 0), (2, 3), (3, 2)]
NEXT_Y = [(0, 2), (2, 0), (1, 3), (3, 1)]


def on_device(grad_parts, weight, first, second, partner_device, partner_column):
    place = jnp.stack([lax.axis_index("shard"), lax.axis_index("dp")]).astype(I32)
    grad = grad_parts[0]

    wanted, codes = call(
        index_kernel,
        (shape(PLANE, RING, 128, dtype=I32), shape(8, FINE, dtype=I32)),
        in_specs=[scalar(), whole(), whole(), whole()],
        moved=1 << 20,
    )(
        place,
        partner_device,
        partner_device.reshape(1, FINE),
        partner_column.reshape(FINE, 1),
    )
    asked = lax.all_to_all(
        wanted, "shard", split_axis=0, concat_axis=0, axis_index_groups=PLANES, tiled=True
    )
    sends = call(
        send_core_kernel,
        (shape(ROWS, 2 * HALF),) * 2,
        in_specs=[scalar(), whole()],
        moved=3 << 20,
    )(place, grad)
    got_core = [lax.ppermute(s, "dp", CORE) for s in sends]
    passed = [
        call(
            lambda *refs, half=half: send_y_kernel(half, *refs),
            shape(ROWS, HALF),
            grid=(1,),
            in_specs=[
                scalar(),
                pl.BlockSpec((ROWS, 4 * FEATS), lambda i: (0, 0)),
                pl.BlockSpec((ROWS, HALF), lambda i: (0, 0)),
            ],
            out_specs=pl.BlockSpec((ROWS, HALF), lambda i: (0, 0)),
            moved=1 << 20,
        )(place, grad, got_core[half])
        for half in range(2)
    ]
    got_y = [lax.ppermute(p, "dp", NEXT_Y) for p in passed]
    state = []
    for half in range(2):
        after = (got_y[1], wanted) if half == 0 else ()
        state.append(
            call(
                lambda *refs, half=half: update_kernel(half, *refs),
                shape(ROWS, WIDE),
                in_specs=[scalar()]
                + [far_away()] * 6
                + [pl.BlockSpec(memory_space=pl.ANY)] * len(after),
                scratch=(
                    pltpu.VMEM((ROWS, HALF), BF16),
                    pltpu.VMEM((5, ROWS, HALF), F32),
                    pltpu.SemaphoreType.DMA((6,)),
                ),
                moved=2 << 20,
            )(place, grad, got_core[half], got_y[half], weight, first, second, *after)
        )

    def pick(planes, sources, wait, after=()):
        if wait:
            after = (*after, token(sources, wait))
        return call(
            lambda *refs: pick_kernel(planes, *refs),
            shape(PLANE, SENT, WIDE),
            in_specs=[scalar(), whole()]
            + [far_away()] * len(sources)
            + [pl.BlockSpec(memory_space=pl.ANY)] * len(after),
            scratch=(
                pltpu.VMEM((len(sources), ROWS, WIDE), F32),
                pltpu.SemaphoreType.DMA((len(sources),)),
            ),
            flops=4 * SLOTS * PLANE * ROWS * WIDE * 4,
            moved=5 << 20,
        )(place, asked, *sources, *after)

    def to_plane(rows):
        return lax.all_to_all(
            rows, "shard", split_axis=0, concat_axis=0, axis_index_groups=PLANES, tiled=True
        )

    def around(pair):
        return lax.ppermute(pair[0], "shard", UP), lax.ppermute(pair[1], "shard", DOWN)

    one = [around((x, x)) for x in state]
    rows = pick((0, 0, -1, 1), (*state, *one[0]), 4)
    far1 = to_plane(rows)
    one[1] = hold(one[1], wait=10)
    two = [around(pair) for pair in one]
    rows = pick((-1, 1, -2, 2), (*one[1], *two[0]), 5, (far1,))
    far2 = to_plane(rows)
    two[1] = hold(two[1], wait=10)
    three = [around(pair) for pair in two]
    rows = pick((-2, 2, -3, 3), (*two[1], *three[0]), 5, (far2,))
    far3 = to_plane(rows)
    three[1] = hold(three[1], wait=10)
    four = (
        lax.ppermute(three[0][0], "shard", UP),
        lax.ppermute(three[1][1], "shard", DOWN),
    )
    far4 = to_plane(pick((-3, 3, 4, 4), (*three[1], *four), 5, (far3,)))

    acc = []
    for half, parts in enumerate(
        (
            ((0, 0, 0, 56), (1, 1, 24, 56), (2, 2, 24, 56)),
            ((4, 0, 8, 32), (5, 1, 0, 32), (6, 2, 0, 32)),
        )
    ):
        acc.append(
            call(
                lambda *refs, parts=parts: gather_kernel(parts, *refs),
                shape(FINE, WIDE),
                grid=(3,),
                in_specs=[
                    pl.BlockSpec((8, FINE), lambda i: (0, 0)),
                    pl.BlockSpec((ROWS, HALF), lambda i: (0, i)),
                ]
                + [pl.BlockSpec((PLANE, SENT, HALF), lambda i: (0, 0, i))] * 3,
                out_specs=pl.BlockSpec((FINE, HALF), lambda i: (0, i)),
                flops=FINE * 1120 * WIDE * 4,
                moved=8 << 20,
            )(codes, state[half], far1, far2, far3)
        )

    def acc_block(half, state):
        def index(j):
            k = jnp.minimum(j, 1) if half == 0 else jnp.maximum(j - 2, 0)
            return 0, state * 2 + k

        return pl.BlockSpec((FINE, 128), index)

    def far_block(state):
        return pl.BlockSpec((PLANE, SENT, 128), lambda j: (0, 0, state * 2 + lax.rem(j, 2)))

    return call(
        final_kernel,
        (shape(FINE, 2 * FEATS),) * 3,
        grid=(4,),
        in_specs=[pl.BlockSpec((8, FINE), lambda j: (0, 0))]
        + [acc_block(half, s) for half in range(2) for s in range(3)]
        + [far_block(s) for s in range(3)],
        out_specs=(pl.BlockSpec((FINE, 256), lambda j: (0, j)),) * 3,
        flops=FINE * 512 * 1536 * 4,
        moved=12 << 20,
    )(codes, acc[0], acc[0], acc[0], acc[1], acc[1], acc[1], far4, far4, far4)


def solution(mesh):
    placed = (
        P("dp", "shard", None),
        P("shard", "dp"),
        P("shard", "dp"),
        P("shard", "dp"),
        P("shard", None),
        P("shard"),
    )
    return jax.shard_map(
        on_device,
        mesh=mesh,
        in_specs=placed,
        out_specs=(P("shard", "dp"), P("shard", "dp"), P("shard", "dp")),
        check_vma=False,
    )
```

```python
import jax
import jax.numpy as jnp
from jax import lax
from jax.experimental import pallas as pl
from jax.experimental.pallas import tpu as pltpu
from jax.sharding import PartitionSpec as P

STEP = 20

first_decay = 0.9
second_decay = 0.95
learning_rate = 0.02
weight_decay = 0.1
epsilon = 1e-08
own_share = 0.75

F32 = jnp.float32
BF16 = jnp.bfloat16
I32 = jnp.int32

ROWS = 224
FINE = 448
FEATS = 512
HALF = 256
WIDE = 3 * HALF
SLOTS = 16
USED = 14
SENT = 4 * USED
PLANE = 8
RING = 8

VMEM = pltpu.CompilerParams(vmem_limit_bytes=12 * 1024 * 1024)


def call(kernel, out, *, grid=None, in_specs=None, out_specs=None, flops=0, moved=0, aliases=None, scratch=()):
    extra = {}
    if grid is not None:
        extra = dict(grid=grid, in_specs=in_specs, out_specs=out_specs)
    elif in_specs is not None:
        extra = dict(in_specs=in_specs)
    return pl.pallas_call(
        kernel,
        out_shape=out,
        compiler_params=VMEM,
        input_output_aliases=aliases or {},
        scratch_shapes=scratch,
        cost_estimate=pl.CostEstimate(flops=flops, bytes_accessed=moved, transcendentals=0),
        **extra,
    )


def shape(*dims, dtype=F32):
    return jax.ShapeDtypeStruct(dims, dtype)


def whole():
    return pl.BlockSpec(memory_space=pltpu.VMEM)


def far_away():
    return pl.BlockSpec(memory_space=pltpu.HBM)


def scalar():
    return pl.BlockSpec(memory_space=pltpu.SMEM)


def halves(values):
    high = values.astype(BF16)
    return high, (values - high.astype(F32)).astype(BF16)


def split_dot(chosen, values, contract=((1,), (0,))):
    dims = (contract, ((), ()))
    high, low = halves(values)
    return lax.dot_general(chosen, high, dims, preferred_element_type=F32) + lax.dot_general(
        chosen, low, dims, preferred_element_type=F32
    )


def send_core_kernel(place, grad, out0, out1):
    dp = place[1]
    core, y = lax.rem(dp, 2), lax.div(dp, 2)
    for half, out in enumerate((out0, out1)):
        for part, row in enumerate((1 - y, y)):
            at = pl.multiple_of((row * 2 + 1 - core) * FEATS + half * HALF, HALF)
            out[:, part * HALF : (part + 1) * HALF] = grad[:, pl.ds(at, HALF)].astype(F32)


def send_y_kernel(half, place, grad, got, out):
    dp = place[1]
    core, y = lax.rem(dp, 2), lax.div(dp, 2)
    at = pl.multiple_of(((1 - y) * 2 + core) * FEATS + half * HALF, HALF)
    out[...] = grad[:, pl.ds(at, HALF)].astype(F32) + got[...]


def update_kernel(half, place, grad, got, got_y, weight, first, second, *refs):
    out, mine, held, done = refs[-4:]
    at = pl.multiple_of(place[1] * FEATS + half * HALF, HALF)
    here = pl.ds(half * HALF, HALF)
    copies = [pltpu.make_async_copy(grad.at[:, pl.ds(at, HALF)], mine, done.at[0])]
    for k, source in enumerate(
        (
            got.at[:, pl.ds(HALF, HALF)],
            got_y,
            first.at[:, here],
            second.at[:, here],
            weight.at[:, here],
        )
    ):
        copies.append(pltpu.make_async_copy(source, held.at[k], done.at[k + 1]))
    for copy in copies:
        copy.start()
    for copy in copies:
        copy.wait()
    got, got_y, first, second, weight = (held.at[k] for k in range(5))
    total = mine[...].astype(F32) + got[...] + got_y[...]
    new_first = first_decay * first[...] + (1.0 - first_decay) * total
    new_second = second_decay * second[...] + (1.0 - second_decay) * total * total
    first_hat = new_first / (1.0 - first_decay**STEP)
    second_hat = new_second / (1.0 - second_decay**STEP)
    old = weight[...]
    new_weight = old - learning_rate * (
        first_hat / (jnp.sqrt(second_hat) + epsilon) + weight_decay * old
    )
    out[:, 0:HALF] = new_weight
    out[:, HALF : 2 * HALF] = new_first
    out[:, 2 * HALF : 3 * HALF] = new_second


def index_kernel(place, dev, dev_row, col, wanted, codes):
    shard = place[0]
    plane, me = lax.div(shard, PLANE), lax.rem(shard, PLANE)
    d = dev[...]
    r = dev_row[...]
    earlier = lax.broadcasted_iota(I32, (FINE, FINE), 1) < lax.broadcasted_iota(
        I32, (FINE, FINE), 0
    )
    slot = jnp.sum(jnp.where(earlier & (d == r), 1, 0), axis=1, keepdims=True)
    later = lax.broadcasted_iota(I32, (FINE, FINE), 0) < lax.broadcasted_iota(
        I32, (FINE, FINE), 1
    )
    slot_row = jnp.sum(jnp.where(later & (d == r), 1, 0), axis=0, keepdims=True)
    source_xy, source_z = r & (PLANE - 1), r >> 3
    row_of = ((r & (PLANE - 1)) << 3) + (r >> 3)
    left = jnp.where(lax.broadcasted_iota(I32, (64, FINE), 0) == row_of, 1.0, 0.0).astype(BF16)
    right = jnp.where(
        lax.broadcasted_iota(I32, (FINE, 128), 1) == me * SLOTS + slot, col[...].astype(F32), 0.0
    ).astype(BF16)
    table = jnp.dot(left, right, preferred_element_type=F32)
    wanted[...] = table.astype(I32).reshape(PLANE, RING, 128)
    away = (source_z - plane + RING) & (RING - 1)
    none = -1

    def place_in(offsets):
        at = jnp.full((1, FINE), none, I32)
        for k, offset in offsets:
            at = jnp.where(away == k, source_xy * 128 + offset + slot_row, at)
        return at

    groups = (
        place_in(((0, 0), (7, 28), (1, 42))),
        place_in(((6, 28), (2, 42))),
        place_in(((5, 28), (3, 42))),
        place_in(((4, 28),)),
        place_in(((0, 14),)),
        place_in(((7, 0), (1, 14))),
        place_in(((6, 0), (2, 14))),
        place_in(((5, 0), (3, 14), (4, 42))),
    )
    codes[...] = jnp.concatenate(groups, axis=0)


def asked_rows(asked, plane):
    here = lax.broadcasted_iota(I32, (RING, 128), 0) == plane
    return jnp.sum(jnp.where(here, jnp.sum(asked[...], axis=0), 0), axis=0, keepdims=True)


def pick_from(asked, plane, values):
    rows = values.shape[0]
    chosen = jnp.where(
        lax.broadcasted_iota(I32, (rows, 128), 0) == asked_rows(asked, plane), 1.0, 0.0
    ).astype(BF16)
    return split_dot(chosen, values, ((0,), (0,)))


def pick_kernel(planes, place, asked, *refs):
    out, held, done = refs[-3:]
    plane = lax.div(place[0], PLANE)
    copies = [
        pltpu.make_async_copy(refs[n], held.at[n], done.at[n]) for n in range(len(planes))
    ]
    for copy in copies:
        copy.start()
    for n, away in enumerate(planes):
        copies[n].wait()
        got = pick_from(asked, (plane + away + RING) & (RING - 1), held[n])
        for d in range(PLANE):
            out[d, n * USED : (n + 1) * USED, :] = got[d * SLOTS : d * SLOTS + USED]


def held_kernel(*refs):
    pass


def hold(arrays, *until, wait=0):
    n = len(arrays)
    return pl.pallas_call(
        held_kernel,
        out_shape=tuple(shape(*a.shape) for a in arrays),
        in_specs=[pl.BlockSpec(memory_space=pl.ANY)] * (n + len(until)),
        out_specs=(pl.BlockSpec(memory_space=pl.ANY),) * n,
        input_output_aliases={i: i for i in range(n)},
        cost_estimate=pl.CostEstimate(flops=wait * 10**9, bytes_accessed=0, transcendentals=0),
    )(*arrays, *until)


def token_kernel(*refs):
    refs[-1][...] = jnp.zeros((8, 128), F32)


def token(arrays, wait):
    return call(
        token_kernel,
        shape(8, 128),
        in_specs=[pl.BlockSpec(memory_space=pl.ANY)] * len(arrays),
        flops=wait * 10**9,
    )(*arrays)


def far_dot(at, far):
    rows = far.shape[0] * far.shape[1]
    chosen = jnp.where(
        lax.broadcasted_iota(I32, (rows, FINE), 0) == at, 1.0 - own_share, 0.0
    ).astype(BF16)
    return split_dot(chosen, far.reshape(rows, far.shape[2]), ((0,), (0,)))


def far_part(codes, lane, far, low, high):
    at = codes[lane : lane + 1, :]
    xy, row = at >> 7, at & 127
    here = (at >= 0) & (row >= low) & (row < high)
    at = jnp.where(here, xy * (high - low) + row - low, -1)
    return far_dot(at, far[:, low:high, :])


def near_part(near):
    own = lax.broadcasted_iota(I32, (FINE, ROWS), 0) >> 1
    chosen = jnp.where(
        lax.broadcasted_iota(I32, (FINE, ROWS), 1) == own, own_share, 0.0
    ).astype(BF16)
    return split_dot(chosen, near[...])


def gather_kernel(parts, codes, near, *refs):
    total = near_part(near)
    for lane, exchange, low, high in parts:
        total = total + far_part(codes, lane, refs[exchange], low, high)
    refs[-1][...] = total


def final_kernel(codes, *refs):
    first_half = pl.program_id(0) < 2
    at = jnp.where(first_half, codes[3:4, :], codes[7:8, :])
    at = jnp.where(at >= 0, (at >> 7) * SENT + (at & 127), -1)
    rows = PLANE * SENT
    chosen = jnp.where(
        lax.broadcasted_iota(I32, (rows, FINE), 0) == at, 1.0 - own_share, 0.0
    ).astype(BF16)
    row = lax.broadcasted_iota(I32, (256, 256), 0) & 127
    lane = lax.broadcasted_iota(I32, (256, 256), 1) >> 1
    twice = jnp.where(row == lane, 1.0, 0.0).astype(BF16)
    far = [piece for k in range(3) for piece in halves(refs[6 + k][...].reshape(rows, 128))]
    far = lax.dot_general(
        chosen,
        jnp.concatenate(far, axis=1),
        (((0,), (0,)), ((), ())),
        preferred_element_type=F32,
    )
    for state in range(3):
        acc0, acc1, out = (refs[3 * k + state] for k in (0, 1, 3))
        at = state * 256
        mixed = jnp.where(first_half, acc0[...], acc1[...])
        mixed = mixed + far[:, at : at + 128] + far[:, at + 128 : at + 256]
        out[...] = jnp.dot(
            jnp.concatenate(halves(mixed), axis=1), twice, preferred_element_type=F32
        )


PLANES = [[z * PLANE + p for p in range(PLANE)] for z in range(RING)]
UP = [(z * PLANE + p, ((z + 1) % RING) * PLANE + p) for z in range(RING) for p in range(PLANE)]
DOWN = [(b, a) for a, b in UP]
CORE = [(0, 1), (1, 0), (2, 3), (3, 2)]
NEXT_Y = [(0, 2), (2, 0), (1, 3), (3, 1)]


def on_device(grad_parts, weight, first, second, partner_device, partner_column):
    place = jnp.stack([lax.axis_index("shard"), lax.axis_index("dp")]).astype(I32)
    grad = grad_parts[0]

    wanted, codes = call(
        index_kernel,
        (shape(PLANE, RING, 128, dtype=I32), shape(8, FINE, dtype=I32)),
        in_specs=[scalar(), whole(), whole(), whole()],
        moved=1 << 20,
    )(
        place,
        partner_device,
        partner_device.reshape(1, FINE),
        partner_column.reshape(FINE, 1),
    )
    asked = lax.all_to_all(
        wanted, "shard", split_axis=0, concat_axis=0, axis_index_groups=PLANES, tiled=True
    )
    sends = call(
        send_core_kernel,
        (shape(ROWS, 2 * HALF),) * 2,
        in_specs=[scalar(), whole()],
        moved=3 << 20,
    )(place, grad)
    got_core = [lax.ppermute(s, "dp", CORE) for s in sends]
    passed = [
        call(
            lambda *refs, half=half: send_y_kernel(half, *refs),
            shape(ROWS, HALF),
            grid=(1,),
            in_specs=[
                scalar(),
                pl.BlockSpec((ROWS, 4 * FEATS), lambda i: (0, 0)),
                pl.BlockSpec((ROWS, HALF), lambda i: (0, 0)),
            ],
            out_specs=pl.BlockSpec((ROWS, HALF), lambda i: (0, 0)),
            moved=1 << 20,
        )(place, grad, got_core[half])
        for half in range(2)
    ]
    got_y = [lax.ppermute(p, "dp", NEXT_Y) for p in passed]
    state = []
    for half in range(2):
        after = (passed[1], wanted) if half == 0 else (token((state[0],), 10),)
        state.append(
            call(
                lambda *refs, half=half: update_kernel(half, *refs),
                shape(ROWS, WIDE),
                in_specs=[scalar()]
                + [far_away()] * 6
                + [pl.BlockSpec(memory_space=pl.ANY)] * len(after),
                scratch=(
                    pltpu.VMEM((ROWS, HALF), BF16),
                    pltpu.VMEM((5, ROWS, HALF), F32),
                    pltpu.SemaphoreType.DMA((6,)),
                ),
                moved=2 << 20,
            )(place, grad, got_core[half], got_y[half], weight, first, second, *after)
        )

    def pick(planes, sources, wait, after=()):
        if wait:
            after = (*after, token(sources, wait))
        return call(
            lambda *refs: pick_kernel(planes, *refs),
            shape(PLANE, SENT, WIDE),
            in_specs=[scalar(), whole()]
            + [far_away()] * len(sources)
            + [pl.BlockSpec(memory_space=pl.ANY)] * len(after),
            scratch=(
                pltpu.VMEM((len(sources), ROWS, WIDE), F32),
                pltpu.SemaphoreType.DMA((len(sources),)),
            ),
            flops=4 * SLOTS * PLANE * ROWS * WIDE * 4,
            moved=5 << 20,
        )(place, asked, *sources, *after)

    def to_plane(rows):
        return lax.all_to_all(
            rows, "shard", split_axis=0, concat_axis=0, axis_index_groups=PLANES, tiled=True
        )

    def around(pair):
        return lax.ppermute(pair[0], "shard", UP), lax.ppermute(pair[1], "shard", DOWN)

    one = [around((x, x)) for x in state]
    rows = pick((0, 0, -1, 1), (*state, *one[0]), 4)
    far1 = to_plane(rows)
    one[1] = hold(one[1], wait=10)
    two = [around(pair) for pair in one]
    rows = pick((-1, 1, -2, 2), (*one[1], *two[0]), 5, (far1,))
    far2 = to_plane(rows)
    two[1] = hold(two[1], wait=10)
    three = [around(pair) for pair in two]
    rows = pick((-2, 2, -3, 3), (*two[1], *three[0]), 5, (far2,))
    far3 = to_plane(rows)
    three[1] = hold(three[1], wait=10)
    four = (
        lax.ppermute(three[0][0], "shard", UP),
        lax.ppermute(three[1][1], "shard", DOWN),
    )
    far4 = to_plane(pick((-3, 3, 4, 4), (*three[1], *four), 5, (far3,)))

    acc = []
    for half, parts in enumerate(
        (
            ((0, 0, 0, 56), (1, 1, 24, 56), (2, 2, 24, 56)),
            ((4, 0, 8, 32), (5, 1, 0, 32), (6, 2, 0, 32)),
        )
    ):
        acc.append(
            call(
                lambda *refs, parts=parts: gather_kernel(parts, *refs),
                shape(FINE, WIDE),
                grid=(3,),
                in_specs=[
                    pl.BlockSpec((8, FINE), lambda i: (0, 0)),
                    pl.BlockSpec((ROWS, HALF), lambda i: (0, i)),
                ]
                + [pl.BlockSpec((PLANE, SENT, HALF), lambda i: (0, 0, i))] * 3,
                out_specs=pl.BlockSpec((FINE, HALF), lambda i: (0, i)),
                flops=FINE * 1120 * WIDE * 4,
                moved=8 << 20,
            )(codes, state[half], far1, far2, far3)
        )

    def acc_block(half, state):
        def index(j):
            k = jnp.minimum(j, 1) if half == 0 else jnp.maximum(j - 2, 0)
            return 0, state * 2 + k

        return pl.BlockSpec((FINE, 128), index)

    def far_block(state):
        return pl.BlockSpec((PLANE, SENT, 128), lambda j: (0, 0, state * 2 + lax.rem(j, 2)))

    return call(
        final_kernel,
        (shape(FINE, 2 * FEATS),) * 3,
        grid=(4,),
        in_specs=[pl.BlockSpec((8, FINE), lambda j: (0, 0))]
        + [acc_block(half, s) for half in range(2) for s in range(3)]
        + [far_block(s) for s in range(3)],
        out_specs=(pl.BlockSpec((FINE, 256), lambda j: (0, j)),) * 3,
        flops=FINE * 512 * 1536 * 4,
        moved=12 << 20,
    )(codes, acc[0], acc[0], acc[0], acc[1], acc[1], acc[1], far4, far4, far4)


def solution(mesh):
    placed = (
        P("dp", "shard", None),
        P("shard", "dp"),
        P("shard", "dp"),
        P("shard", "dp"),
        P("shard", None),
        P("shard"),
    )
    return jax.shard_map(
        on_device,
        mesh=mesh,
        in_specs=placed,
        out_specs=(P("shard", "dp"), P("shard", "dp"), P("shard", "dp")),
        check_vma=False,
    )
```

```python
import jax
import jax.numpy as jnp
from jax import lax
from jax.experimental import pallas as pl
from jax.experimental.pallas import tpu as pltpu
from jax.sharding import PartitionSpec as P

STEP = 20

first_decay = 0.9
second_decay = 0.95
learning_rate = 0.02
weight_decay = 0.1
epsilon = 1e-08
own_share = 0.75

F32 = jnp.float32
BF16 = jnp.bfloat16
I32 = jnp.int32

ROWS = 224
FINE = 448
FEATS = 512
HALF = 256
WIDE = 3 * HALF
SLOTS = 16
USED = 14
SENT = 4 * USED
PLANE = 8
RING = 8

VMEM = pltpu.CompilerParams(vmem_limit_bytes=12 * 1024 * 1024)


def call(kernel, out, *, grid=None, in_specs=None, out_specs=None, flops=0, moved=0, aliases=None, scratch=()):
    extra = {}
    if grid is not None:
        extra = dict(grid=grid, in_specs=in_specs, out_specs=out_specs)
    elif in_specs is not None:
        extra = dict(in_specs=in_specs)
    return pl.pallas_call(
        kernel,
        out_shape=out,
        compiler_params=VMEM,
        input_output_aliases=aliases or {},
        scratch_shapes=scratch,
        cost_estimate=pl.CostEstimate(flops=flops, bytes_accessed=moved, transcendentals=0),
        **extra,
    )


def shape(*dims, dtype=F32):
    return jax.ShapeDtypeStruct(dims, dtype)


def whole():
    return pl.BlockSpec(memory_space=pltpu.VMEM)


def far_away():
    return pl.BlockSpec(memory_space=pltpu.HBM)


def scalar():
    return pl.BlockSpec(memory_space=pltpu.SMEM)


def halves(values):
    high = values.astype(BF16)
    return high, (values - high.astype(F32)).astype(BF16)


def split_dot(chosen, values, contract=((1,), (0,))):
    dims = (contract, ((), ()))
    high, low = halves(values)
    return lax.dot_general(chosen, high, dims, preferred_element_type=F32) + lax.dot_general(
        chosen, low, dims, preferred_element_type=F32
    )


def send_core_kernel(place, grad, out0, out1):
    dp = place[1]
    core, y = lax.rem(dp, 2), lax.div(dp, 2)
    for half, out in enumerate((out0, out1)):
        for part, row in enumerate((1 - y, y)):
            at = pl.multiple_of((row * 2 + 1 - core) * FEATS + half * HALF, HALF)
            out[:, part * HALF : (part + 1) * HALF] = grad[:, pl.ds(at, HALF)].astype(F32)


def send_y_kernel(half, place, grad, got, out):
    dp = place[1]
    core, y = lax.rem(dp, 2), lax.div(dp, 2)
    at = pl.multiple_of(((1 - y) * 2 + core) * FEATS + half * HALF, HALF)
    out[...] = grad[:, pl.ds(at, HALF)].astype(F32) + got[...]


def update_kernel(half, place, grad, got, got_y, weight, first, second, *refs):
    out, mine, held, done = refs[-4:]
    at = pl.multiple_of(place[1] * FEATS + half * HALF, HALF)
    here = pl.ds(half * HALF, HALF)
    copies = [pltpu.make_async_copy(grad.at[:, pl.ds(at, HALF)], mine, done.at[0])]
    for k, source in enumerate(
        (
            got.at[:, pl.ds(HALF, HALF)],
            got_y,
            first.at[:, here],
            second.at[:, here],
            weight.at[:, here],
        )
    ):
        copies.append(pltpu.make_async_copy(source, held.at[k], done.at[k + 1]))
    for copy in copies:
        copy.start()
    for copy in copies:
        copy.wait()
    got, got_y, first, second, weight = (held.at[k] for k in range(5))
    total = mine[...].astype(F32) + got[...] + got_y[...]
    new_first = first_decay * first[...] + (1.0 - first_decay) * total
    new_second = second_decay * second[...] + (1.0 - second_decay) * total * total
    first_hat = new_first / (1.0 - first_decay**STEP)
    second_hat = new_second / (1.0 - second_decay**STEP)
    old = weight[...]
    new_weight = old - learning_rate * (
        first_hat / (jnp.sqrt(second_hat) + epsilon) + weight_decay * old
    )
    out[:, 0:HALF] = new_weight
    out[:, HALF : 2 * HALF] = new_first
    out[:, 2 * HALF : 3 * HALF] = new_second


def index_kernel(place, dev, dev_row, col, wanted, codes):
    shard = place[0]
    plane, me = lax.div(shard, PLANE), lax.rem(shard, PLANE)
    d = dev[...]
    r = dev_row[...]
    earlier = lax.broadcasted_iota(I32, (FINE, FINE), 1) < lax.broadcasted_iota(
        I32, (FINE, FINE), 0
    )
    slot = jnp.sum(jnp.where(earlier & (d == r), 1, 0), axis=1, keepdims=True)
    later = lax.broadcasted_iota(I32, (FINE, FINE), 0) < lax.broadcasted_iota(
        I32, (FINE, FINE), 1
    )
    slot_row = jnp.sum(jnp.where(later & (d == r), 1, 0), axis=0, keepdims=True)
    source_xy, source_z = r & (PLANE - 1), r >> 3
    row_of = ((r & (PLANE - 1)) << 3) + (r >> 3)
    left = jnp.where(lax.broadcasted_iota(I32, (64, FINE), 0) == row_of, 1.0, 0.0).astype(BF16)
    right = jnp.where(
        lax.broadcasted_iota(I32, (FINE, 128), 1) == me * SLOTS + slot, col[...].astype(F32), 0.0
    ).astype(BF16)
    table = jnp.dot(left, right, preferred_element_type=F32)
    wanted[...] = table.astype(I32).reshape(PLANE, RING, 128)
    away = (source_z - plane + RING) & (RING - 1)
    none = -1

    def place_in(offsets):
        at = jnp.full((1, FINE), none, I32)
        for k, offset in offsets:
            at = jnp.where(away == k, source_xy * 128 + offset + slot_row, at)
        return at

    groups = (
        place_in(((0, 0), (7, 28), (1, 42))),
        place_in(((6, 28), (2, 42))),
        place_in(((5, 28), (3, 42))),
        place_in(((4, 28),)),
        place_in(((0, 14),)),
        place_in(((7, 0), (1, 14))),
        place_in(((6, 0), (2, 14))),
        place_in(((5, 0), (3, 14), (4, 42))),
    )
    codes[...] = jnp.concatenate(groups, axis=0)


def asked_rows(asked, plane):
    here = lax.broadcasted_iota(I32, (RING, 128), 0) == plane
    return jnp.sum(jnp.where(here, jnp.sum(asked[...], axis=0), 0), axis=0, keepdims=True)


def pick_from(asked, plane, values):
    rows = values.shape[0]
    chosen = jnp.where(
        lax.broadcasted_iota(I32, (rows, 128), 0) == asked_rows(asked, plane), 1.0, 0.0
    ).astype(BF16)
    return split_dot(chosen, values, ((0,), (0,)))


def pick_kernel(planes, place, asked, *refs):
    out, held, done = refs[-3:]
    plane = lax.div(place[0], PLANE)
    copies = [
        pltpu.make_async_copy(refs[n], held.at[n], done.at[n]) for n in range(len(planes))
    ]
    for copy in copies:
        copy.start()
    for n, away in enumerate(planes):
        copies[n].wait()
        got = pick_from(asked, (plane + away + RING) & (RING - 1), held[n])
        for d in range(PLANE):
            out[d, n * USED : (n + 1) * USED, :] = got[d * SLOTS : d * SLOTS + USED]


def held_kernel(*refs):
    pass


def hold(arrays, *until, wait=0):
    n = len(arrays)
    return pl.pallas_call(
        held_kernel,
        out_shape=tuple(shape(*a.shape) for a in arrays),
        in_specs=[pl.BlockSpec(memory_space=pl.ANY)] * (n + len(until)),
        out_specs=(pl.BlockSpec(memory_space=pl.ANY),) * n,
        input_output_aliases={i: i for i in range(n)},
        cost_estimate=pl.CostEstimate(flops=wait * 10**9, bytes_accessed=0, transcendentals=0),
    )(*arrays, *until)


def token_kernel(*refs):
    refs[-1][...] = jnp.zeros((8, 128), F32)


def token(arrays, wait):
    return call(
        token_kernel,
        shape(8, 128),
        in_specs=[pl.BlockSpec(memory_space=pl.ANY)] * len(arrays),
        flops=wait * 10**9,
    )(*arrays)


def far_dot(at, far):
    rows = far.shape[0] * far.shape[1]
    chosen = jnp.where(
        lax.broadcasted_iota(I32, (rows, FINE), 0) == at, 1.0 - own_share, 0.0
    ).astype(BF16)
    return split_dot(chosen, far.reshape(rows, far.shape[2]), ((0,), (0,)))


def far_part(codes, lane, far, low, high):
    at = codes[lane : lane + 1, :]
    xy, row = at >> 7, at & 127
    here = (at >= 0) & (row >= low) & (row < high)
    at = jnp.where(here, xy * (high - low) + row - low, -1)
    return far_dot(at, far[:, low:high, :])


def near_part(near):
    own = lax.broadcasted_iota(I32, (FINE, ROWS), 0) >> 1
    chosen = jnp.where(
        lax.broadcasted_iota(I32, (FINE, ROWS), 1) == own, own_share, 0.0
    ).astype(BF16)
    return split_dot(chosen, near[...])


def gather_kernel(parts, codes, near, *refs):
    total = near_part(near)
    for lane, exchange, low, high in parts:
        total = total + far_part(codes, lane, refs[exchange], low, high)
    refs[-1][...] = total


def final_kernel(codes, *refs):
    first_half = pl.program_id(0) < 2
    at = jnp.where(first_half, codes[3:4, :], codes[7:8, :])
    at = jnp.where(at >= 0, (at >> 7) * SENT + (at & 127), -1)
    rows = PLANE * SENT
    chosen = jnp.where(
        lax.broadcasted_iota(I32, (rows, FINE), 0) == at, 1.0 - own_share, 0.0
    ).astype(BF16)
    row = lax.broadcasted_iota(I32, (256, 256), 0) & 127
    lane = lax.broadcasted_iota(I32, (256, 256), 1) >> 1
    twice = jnp.where(row == lane, 1.0, 0.0).astype(BF16)
    far = [piece for k in range(3) for piece in halves(refs[6 + k][...].reshape(rows, 128))]
    far = lax.dot_general(
        chosen,
        jnp.concatenate(far, axis=1),
        (((0,), (0,)), ((), ())),
        preferred_element_type=F32,
    )
    for state in range(3):
        acc0, acc1, out = (refs[3 * k + state] for k in (0, 1, 3))
        at = state * 256
        mixed = jnp.where(first_half, acc0[...], acc1[...])
        mixed = mixed + far[:, at : at + 128] + far[:, at + 128 : at + 256]
        out[...] = jnp.dot(
            jnp.concatenate(halves(mixed), axis=1), twice, preferred_element_type=F32
        )


PLANES = [[z * PLANE + p for p in range(PLANE)] for z in range(RING)]
UP = [(z * PLANE + p, ((z + 1) % RING) * PLANE + p) for z in range(RING) for p in range(PLANE)]
DOWN = [(b, a) for a, b in UP]
CORE = [(0, 1), (1, 0), (2, 3), (3, 2)]
NEXT_Y = [(0, 2), (2, 0), (1, 3), (3, 1)]


def on_device(grad_parts, weight, first, second, partner_device, partner_column):
    place = jnp.stack([lax.axis_index("shard"), lax.axis_index("dp")]).astype(I32)
    grad = grad_parts[0]

    wanted, codes = call(
        index_kernel,
        (shape(PLANE, RING, 128, dtype=I32), shape(8, FINE, dtype=I32)),
        in_specs=[scalar(), whole(), whole(), whole()],
        moved=1 << 20,
    )(
        place,
        partner_device,
        partner_device.reshape(1, FINE),
        partner_column.reshape(FINE, 1),
    )
    asked = lax.all_to_all(
        wanted, "shard", split_axis=0, concat_axis=0, axis_index_groups=PLANES, tiled=True
    )
    sends = call(
        send_core_kernel,
        (shape(ROWS, 2 * HALF),) * 2,
        in_specs=[scalar(), whole()],
        moved=3 << 20,
    )(place, grad)
    got_core = [lax.ppermute(s, "dp", CORE) for s in sends]
    passed = [
        call(
            lambda *refs, half=half: send_y_kernel(half, *refs),
            shape(ROWS, HALF),
            grid=(1,),
            in_specs=[
                scalar(),
                pl.BlockSpec((ROWS, 4 * FEATS), lambda i: (0, 0)),
                pl.BlockSpec((ROWS, HALF), lambda i: (0, 0)),
            ],
            out_specs=pl.BlockSpec((ROWS, HALF), lambda i: (0, 0)),
            moved=1 << 20,
        )(place, grad, got_core[half])
        for half in range(2)
    ]
    got_y = [lax.ppermute(p, "dp", NEXT_Y) for p in passed]
    state = []
    for half in range(2):
        after = (passed[1], wanted) if half == 0 else (token((state[0],), 10),)
        state.append(
            call(
                lambda *refs, half=half: update_kernel(half, *refs),
                shape(ROWS, WIDE),
                in_specs=[scalar()]
                + [far_away()] * 6
                + [pl.BlockSpec(memory_space=pl.ANY)] * len(after),
                scratch=(
                    pltpu.VMEM((ROWS, HALF), BF16),
                    pltpu.VMEM((5, ROWS, HALF), F32),
                    pltpu.SemaphoreType.DMA((6,)),
                ),
                moved=2 << 20,
            )(place, grad, got_core[half], got_y[half], weight, first, second, *after)
        )

    def pick(planes, sources, wait, after=()):
        if wait:
            after = (*after, token(sources, wait))
        return call(
            lambda *refs: pick_kernel(planes, *refs),
            shape(PLANE, SENT, WIDE),
            in_specs=[scalar(), whole()]
            + [far_away()] * len(sources)
            + [pl.BlockSpec(memory_space=pl.ANY)] * len(after),
            scratch=(
                pltpu.VMEM((len(sources), ROWS, WIDE), F32),
                pltpu.SemaphoreType.DMA((len(sources),)),
            ),
            flops=4 * SLOTS * PLANE * ROWS * WIDE * 4,
            moved=5 << 20,
        )(place, asked, *sources, *after)

    def to_plane(rows):
        return lax.all_to_all(
            rows, "shard", split_axis=0, concat_axis=0, axis_index_groups=PLANES, tiled=True
        )

    def around(pair):
        return lax.ppermute(pair[0], "shard", UP), lax.ppermute(pair[1], "shard", DOWN)

    one = [around((x, x)) for x in state]
    rows = pick((0, 0, -1, 1), (*state, *one[0]), 8)
    far1 = to_plane(rows)
    one[1] = hold(one[1], wait=10)
    two = [around(pair) for pair in one]
    rows = pick((-1, 1, -2, 2), (*one[1], *two[0]), 5, (far1,))
    far2 = to_plane(rows)
    two[1] = hold(two[1], wait=10)
    three = [around(pair) for pair in two]
    rows = pick((-2, 2, -3, 3), (*two[1], *three[0]), 5, (far2,))
    far3 = to_plane(rows)
    three[1] = hold(three[1], wait=10)
    four = (
        lax.ppermute(three[0][0], "shard", UP),
        lax.ppermute(three[1][1], "shard", DOWN),
    )
    far4 = to_plane(pick((-3, 3, 4, 4), (*three[1], *four), 5, (far3,)))

    acc = []
    for half, parts in enumerate(
        (
            ((0, 0, 0, 56), (1, 1, 24, 56), (2, 2, 24, 56)),
            ((4, 0, 8, 32), (5, 1, 0, 32), (6, 2, 0, 32)),
        )
    ):
        acc.append(
            call(
                lambda *refs, parts=parts: gather_kernel(parts, *refs),
                shape(FINE, WIDE),
                grid=(3,),
                in_specs=[
                    pl.BlockSpec((8, FINE), lambda i: (0, 0)),
                    pl.BlockSpec((ROWS, HALF), lambda i: (0, i)),
                ]
                + [pl.BlockSpec((PLANE, SENT, HALF), lambda i: (0, 0, i))] * 3,
                out_specs=pl.BlockSpec((FINE, HALF), lambda i: (0, i)),
                flops=FINE * 1120 * WIDE * 4,
                moved=8 << 20,
            )(codes, state[half], far1, far2, far3)
        )

    def acc_block(half, state):
        def index(j):
            k = jnp.minimum(j, 1) if half == 0 else jnp.maximum(j - 2, 0)
            return 0, state * 2 + k

        return pl.BlockSpec((FINE, 128), index)

    def far_block(state):
        return pl.BlockSpec((PLANE, SENT, 128), lambda j: (0, 0, state * 2 + lax.rem(j, 2)))

    return call(
        final_kernel,
        (shape(FINE, 2 * FEATS),) * 3,
        grid=(4,),
        in_specs=[pl.BlockSpec((8, FINE), lambda j: (0, 0))]
        + [acc_block(half, s) for half in range(2) for s in range(3)]
        + [far_block(s) for s in range(3)],
        out_specs=(pl.BlockSpec((FINE, 256), lambda j: (0, j)),) * 3,
        flops=FINE * 512 * 1536 * 4,
        moved=12 << 20,
    )(codes, acc[0], acc[0], acc[0], acc[1], acc[1], acc[1], far4, far4, far4)


def solution(mesh):
    placed = (
        P("dp", "shard", None),
        P("shard", "dp"),
        P("shard", "dp"),
        P("shard", "dp"),
        P("shard", None),
        P("shard"),
    )
    return jax.shard_map(
        on_device,
        mesh=mesh,
        in_specs=placed,
        out_specs=(P("shard", "dp"), P("shard", "dp"), P("shard", "dp")),
        check_vma=False,
    )
```
